32 devices in a mesh: groups: 2 (over y), seq: 4 (over z), tp: 4 (over x, core).
Axes of the slice: x: 2, y: 2, z: 4, core: 2. Of those that a mesh axis runs over, the one named last changes fastest.
Arguments:
- branches: bfloat16 [1024, 3, 2048], P(('groups', 'seq'), None, 'tp'), parts along dimension 0, may hold values from -5 to 5
- residual: bfloat16 [1024, 4096], P(('groups', 'seq'), 'tp'), parts along dimension 0, may hold values from -32 to 32
- segments: int32 [1024], P('groups'), parts along dimension 0, may hold values from 0 to 7, never falling along the last dimension, each value on 1 to 256 neighbouring positions
- long_filter: float32 [512, 2048], P('seq', 'tp'), may hold values from -4 to 4
- short_taps: float32 [3, 3, 2048], P(None, None, 'tp'), may hold values from -3 to 3
- skip_gain: float32 [2048], P('tp'), may hold values from -3 to 3
- out_weight: bfloat16 [2048, 4096], P(None, 'tp'), may hold values from -0.125 to 0.125
- norm_gain: float32 [4096], replicated, may hold values from 0.1 to 1.9
- head_weight: bfloat16 [4096, 3, 2048], P(None, None, 'tp'), may hold values from -27 to 27
Outputs:
- hidden: bfloat16 [1024, 4096], P(('groups', 'seq'), 'tp'), parts along dimension 0
- context: bfloat16 [1024, 2048], P(('groups', 'seq'), 'tp'), parts along dimension 0
The draws below stay inside these ranges and needn't reach their ends.
There are 2 independent parts, one for each index of `groups`. The reference program is written for one: setup_inputs(seed, part) draws one part's arguments, and reference() takes and returns one part's arrays. A program takes and returns all parts, laid end to end along the dimension named above; an argument that names none is the same for every part. Nothing has to cross between parts.
Inputs may be any that keep to these rules, and one draw needn't show every extreme that they name: `segments`: document ids never fall along the window; a document holds 1 to 256 positions, and one holds exactly 256.
All inputs are finite; a program needn't handle non-finite values.
Results may differ from the reference program's by a relative error of at most 0.017.
Values may be sent and summed in bfloat16 or wider, within the bound.
A program may use at most 64 MiB of HBM per device.

```python
import math
import jax
import jax.numpy as jnp
import numpy as np
from jax import lax

D = 4096
C = 2048
H = 16
DH = 128
S_DEV = 128
L = 512


def draw_residual(key, part):
    keys = jax.random.split(jax.random.fold_in(key, 11), 3)
    rows = jnp.exp(jax.random.uniform(keys[0], (L, 1), minval=math.log(0.4), maxval=math.log(2.0)))
    rising = 3.0 ** (jnp.arange(D, dtype=jnp.float32) / D)
    spread = jnp.exp(jax.random.uniform(keys[1], (1, D), minval=math.log(0.5), maxval=math.log(2.0)))
    noise = jnp.clip(jax.random.normal(keys[2], (L, D)), -4.0, 4.0)
    values = noise * rows * rising[None, :] * spread / 1.5
    return values.astype(jnp.bfloat16)


def draw_long_filter(key, part):
    keys = jax.random.split(jax.random.fold_in(key, 23), 6)
    share = 0.5
    fast_life = jnp.exp(jax.random.uniform(keys[0], (C,), minval=math.log(S_DEV / 8.0), maxval=math.log(L / 2.0)))
    slow_life = jnp.exp(jax.random.uniform(keys[1], (C,), minval=math.log(2.0 * L), maxval=math.log(8.0 * L)))
    is_slow = jax.random.uniform(keys[2], (C,)) < share
    life = jnp.where(is_slow, slow_life, fast_life)
    time_steps = jnp.arange(L, dtype=jnp.float32)[:, None]
    decay_envelope = jnp.exp(-time_steps / life[None, :])
    spike_locations = jax.random.randint(keys[3], (2, C), 1, L)
    dropped_entries = jax.random.uniform(keys[4], (2, C), minval=0.5, maxval=0.8)
    for spike_signal in range(2):
        decay_envelope = decay_envelope * jnp.where(time_steps >= spike_locations[spike_signal][None, :].astype(jnp.float32), dropped_entries[spike_signal][None, :], 1.0)
    rough = jnp.clip(jax.random.normal(keys[5], (L, C)), -4.0, 4.0)
    norm = jnp.sqrt(jnp.sum(decay_envelope * decay_envelope, axis=0, keepdims=True))
    return (decay_envelope * rough / norm).astype(jnp.float32)


def draw_head_weight(key, part):
    keys = jax.random.split(jax.random.fold_in(key, 37), 1)
    weight = jnp.clip(jax.random.normal(keys[0], (D, 3, H * DH)), -4.0, 4.0) / math.sqrt(D)
    return weight.astype(jnp.bfloat16)


def shard_levels(own_key, dims, cuts, low, high):
    def one(axis_at, blocks):
        heights = jax.random.uniform(jax.random.fold_in(jax.random.fold_in(own_key, 6), axis_at), (blocks,), jnp.float32, low / len(cuts), high / len(cuts))
        return jnp.repeat(jnp.exp(heights), dims[axis_at] // blocks).reshape((-1,) + (1,) * (len(dims) - axis_at - 1))

    level = one(*cuts[0])
    for cut in cuts[1:]:
        level = level * one(*cut)
    return level


def profile(count, total, most, lean):
    loads = [(1 << 20) // math.isqrt(grade ** lean) + 1 for grade in range(2, count + 1)]
    spare, counts = total - most - (count - 1), [1] * (count - 1)
    while spare > 0:
        free = [i for i in range(count - 1) if counts[i] < most]
        whole, budget = sum([loads[i] for i in free]), spare
        for i in free:
            addition = min(most - counts[i], max(1, budget * loads[i] // whole), spare)
            counts[i] = counts[i] + addition
            spare = spare - addition
    return np.array([most] + counts)


def ragged_sizes(rng, number_of, total, reach, skew):
    if number_of == 2:
        one = jax.random.randint(rng, (), max(1, total - reach), min(reach, total - 1) + 1)
        return jnp.stack([one, total - one])
    sizes = jnp.asarray(profile(number_of, total, reach, skew), jnp.int32)
    couples = (number_of - 1) // 2
    source_of, taker = sizes[1:1 + 2 * couples:2], sizes[2:2 + 2 * couples:2]
    room = jnp.minimum(source_of - 1, reach - taker)
    shifted = jax.random.randint(jax.random.fold_in(rng, 1), (couples,), 0, 1 << 20) % (room + 1)
    sizes = sizes.at[1:1 + 2 * couples:2].set(source_of - shifted).at[2:2 + 2 * couples:2].set(taker + shifted)
    return sizes[jax.random.permutation(jax.random.fold_in(rng, 2), number_of)]


def scatter_about(stream_key, dims, width, most, shards=(), held_as=jnp.bfloat16):
    entries = jax.random.normal(stream_key, dims, jnp.float32) * width
    if len(shards) > 0:
        entries = shard_levels(stream_key, dims, shards, -0.22, 0.18) * entries
    return jnp.clip(entries, min=-most, max=most).astype(held_as)


def setup_inputs(seed: int = 0, part: int = 0) -> dict:
    seeds = jax.random.split(jax.random.key(seed), 10)
    part_splits = jax.random.split(jax.random.fold_in(seeds[9], part), 10)
    return {
        "branches": scatter_about(part_splits[0], (L, 3, C), 1.0, 5.0, ((0, 4), (2, 4))),
        "residual": draw_residual(jax.random.fold_in(jax.random.fold_in(seeds[9], part), 71), part),
        "segments": jnp.searchsorted(jnp.cumsum(ragged_sizes(part_splits[2], 8, L, L // 2, 0)), jnp.arange(L), side="right").astype(jnp.int32),
        "long_filter": draw_long_filter(jax.random.fold_in(seeds[9], 71), part),
        "short_taps": scatter_about(seeds[4], (3, 3, C), 0.6, 3.0, ((2, 4),), jnp.float32),
        "skip_gain": scatter_about(seeds[5], (C,), 1.0, 3.0, ((0, 4),), jnp.float32),
        "out_weight": scatter_about(seeds[6], (C, D), C ** -0.5, 0.125, ((1, 4),)),
        "norm_gain": jnp.clip(1.0 + 0.18 * jax.random.normal(seeds[7], (D,), jnp.float32), 0.1, 1.9),
        "head_weight": draw_head_weight(jax.random.fold_in(seeds[9], 71), part),
    }


EPSILON = 1e-05

def featurize(branches, short_taps, segments):
    values = branches.astype(jnp.float32)
    flagged_positions = jnp.concatenate([jnp.full((2,), -1, jnp.int32), segments.astype(jnp.int32)])
    padded = jnp.concatenate([jnp.zeros((2, 3, C), jnp.float32), values], axis=0)
    featured = jnp.zeros((L, 3, C), jnp.float32)
    for offset in range(3):
        earlier = padded[2 - offset:2 - offset + L]
        same = flagged_positions[2 - offset:2 - offset + L] == segments
        featured = featured + jnp.where(same[:, None, None], short_taps[:, offset, :][None] * earlier, 0.0)
    return featured

def reference(branches, residual, segments, long_filter, short_taps, skip_gain, out_weight, norm_gain, head_weight):
    featured = featurize(branches, short_taps, segments)
    mixed = featured[:, 1] * featured[:, 2]
    spectrum = jnp.fft.rfft(mixed, n=2 * L, axis=0) * jnp.fft.rfft(long_filter, n=2 * L, axis=0)
    conv = jnp.fft.irfft(spectrum, n=2 * L, axis=0)[:L]
    gated = (featured[:, 0] * (conv + skip_gain * mixed)).astype(jnp.bfloat16)
    mixed_out = jnp.dot(gated, out_weight, preferred_element_type=jnp.float32)
    hidden = (residual.astype(jnp.float32) + mixed_out).astype(jnp.bfloat16)
    wide = hidden.astype(jnp.float32)
    scale = lax.rsqrt(lax.optimization_barrier(jnp.mean(wide * wide, axis=1)) + EPSILON)
    normed = (wide * scale[:, None] * norm_gain).astype(jnp.bfloat16)
    projected = jnp.dot(normed, head_weight.reshape(D, 3 * H * DH), preferred_element_type=jnp.float32).astype(jnp.bfloat16)
    projected = projected.reshape(L, 3, H, DH).transpose(1, 2, 0, 3)
    positions = jnp.arange(L, dtype=jnp.int32)
    allowed = (positions[None, :] <= positions[:, None]) & (segments[None, :] == segments[:, None])
    factor = 1.0 / math.sqrt(DH)

    def one_head(operands):
        query, keys, values = operands
        score = jnp.dot(query, keys.T, preferred_element_type=jnp.float32) * factor
        peak = lax.optimization_barrier(jnp.max(jnp.where(allowed, score, -1e+30), axis=1, keepdims=True))
        weight = jnp.where(allowed, jnp.exp(score - peak), 0.0)
        mass = lax.optimization_barrier(jnp.sum(weight, axis=1, keepdims=True))
        total = jnp.dot(weight.astype(jnp.bfloat16), values, preferred_element_type=jnp.float32)
        return total / mass
    context = lax.map(one_head, (projected[0], projected[1], projected[2]))
    context = context.transpose(1, 0, 2).reshape(L, H * DH).astype(jnp.bfloat16)
    return (hidden, context)
```

```python
import math

import jax
import ml_dtypes
import numpy as np
import jax.numpy as jnp
from jax import lax
from jax.sharding import PartitionSpec as P

DH = 128


EPSILON = 1e-05
HIGHEST = lax.Precision.HIGHEST
TWO_PI = 2.0 * math.pi


def passed_along(array, axis, by):
    count = lax.axis_size(axis)
    pairs = [(i, i + by) for i in range(count) if 0 <= i + by < count]
    return lax.ppermute(array, axis, pairs)


def complex_times(left_real, left_imag, right_real, right_imag):
    return (
        left_real * right_real - left_imag * right_imag,
        left_real * right_imag + left_imag * right_real,
    )


def window_convolve(whole, shards):
    count = whole.shape[1]
    rows = count // shards
    span = 2 * shards
    total = 2 * count
    data = whole.reshape(2, shards, rows, whole.shape[2])
    outer_index = jnp.arange(span, dtype=jnp.int32)
    block_index = jnp.arange(shards, dtype=jnp.int32)
    place_index = jnp.arange(rows, dtype=jnp.int32)
    outer = TWO_PI * (outer_index[:, None] * block_index[None, :] % span).astype(jnp.float32) / span
    outer_cos = jnp.cos(outer)
    outer_sin = jnp.sin(outer)
    first_real = jnp.einsum("ka,sabc->skbc", outer_cos, data, precision=HIGHEST)
    first_imag = -jnp.einsum("ka,sabc->skbc", outer_sin, data, precision=HIGHEST)
    twist = (
        TWO_PI * (outer_index[:, None] * place_index[None, :] % total).astype(jnp.float32) / total
    )
    twist_cos = jnp.cos(twist)[:, :, None]
    twist_sin = jnp.sin(twist)[:, :, None]
    turned_real, turned_imag = complex_times(first_real, first_imag, twist_cos, -twist_sin)
    inner = TWO_PI * (place_index[:, None] * place_index[None, :] % rows).astype(jnp.float32) / rows
    inner_cos = jnp.cos(inner)
    inner_sin = jnp.sin(inner)
    spec_real = jnp.einsum("bq,skbc->skqc", inner_cos, turned_real, precision=HIGHEST) + jnp.einsum(
        "bq,skbc->skqc", inner_sin, turned_imag, precision=HIGHEST
    )
    spec_imag = jnp.einsum("bq,skbc->skqc", inner_cos, turned_imag, precision=HIGHEST) - jnp.einsum(
        "bq,skbc->skqc", inner_sin, turned_real, precision=HIGHEST
    )
    prod_real, prod_imag = complex_times(spec_real[0], spec_imag[0], spec_real[1], spec_imag[1])
    back_real = jnp.einsum("qb,kqc->kbc", inner_cos, prod_real, precision=HIGHEST) - jnp.einsum(
        "qb,kqc->kbc", inner_sin, prod_imag, precision=HIGHEST
    )
    back_imag = jnp.einsum("qb,kqc->kbc", inner_cos, prod_imag, precision=HIGHEST) + jnp.einsum(
        "qb,kqc->kbc", inner_sin, prod_real, precision=HIGHEST
    )
    reverted_real, reverted_imag = complex_times(back_real, back_imag, twist_cos, twist_sin)
    result = jnp.einsum("ka,kbc->abc", outer_cos, reverted_real, precision=HIGHEST) - jnp.einsum(
        "ka,kbc->abc", outer_sin, reverted_imag, precision=HIGHEST
    )
    return (result / total).reshape(count, whole.shape[2])


def local(
    branches,
    residual,
    segments,
    long_filter,
    short_taps,
    skip_gain,
    out_weight,
    norm_gain,
    head_weight,
):
    rows = branches.shape[0]
    channels = branches.shape[2]
    shards = lax.axis_size("seq")
    rank = lax.axis_index("seq")
    first = rank * rows
    prior = passed_along(branches[rows - 2 :], "seq", 1)
    padded = jnp.concatenate([prior, branches], axis=0).astype(jnp.float32)
    flagged_positions = jnp.concatenate([jnp.full((2,), -1, jnp.int32), segments])
    window = lax.dynamic_slice_in_dim(flagged_positions, first, rows + 2)
    own_ids = window[2:]
    featured = jnp.zeros((rows, 3, channels), jnp.float32)
    for offset in range(3):
        earlier = padded[2 - offset : 2 - offset + rows]
        same = window[2 - offset : 2 - offset + rows] == own_ids
        featured = featured + jnp.where(
            same[:, None, None], short_taps[:, offset, :][None] * earlier, 0.0
        )
    mixed = featured[:, 1] * featured[:, 2]
    signals = jnp.stack([mixed, long_filter])
    whole = lax.all_to_all(signals, "seq", split_axis=2, concat_axis=1, tiled=True)
    columns = window_convolve(whole, shards)
    conv = lax.all_to_all(columns, "seq", split_axis=0, concat_axis=1, tiled=True)
    gated = (featured[:, 0] * (conv + skip_gain * mixed)).astype(jnp.bfloat16)
    weight_rows = out_weight
    mixed_out = jnp.dot(
        lax.all_gather(gated, "tp", axis=1, tiled=True),
        weight_rows,
        preferred_element_type=jnp.float32,
    )
    hidden = (residual.astype(jnp.float32) + mixed_out).astype(jnp.bfloat16)
    width = head_weight.shape[0]
    flat_weight = head_weight.reshape(width, -1)
    local_wide = hidden.astype(jnp.float32)
    squares = jnp.sum(local_wide * local_wide, axis=1)
    total_squares = lax.psum(squares, "tp")
    scale = lax.rsqrt(total_squares / width + EPSILON)
    local_width = hidden.shape[1]
    local_gain = lax.dynamic_slice_in_dim(
        norm_gain, lax.axis_index("tp") * local_width, local_width
    )
    normed = (local_wide * scale[:, None] * local_gain).astype(jnp.bfloat16)
    weight_rows = flat_weight
    projected = jnp.dot(
        lax.all_gather(normed, "tp", axis=1, tiled=True),
        weight_rows,
        preferred_element_type=jnp.float32,
    )
    projected = projected.astype(jnp.bfloat16).reshape(rows, 3, -1, DH)
    query = projected[:, 0]
    keys = projected[:, 1]
    values = projected[:, 2]
    local_heads = query.shape[1]
    factor = 1.0 / math.sqrt(DH)
    query_pos = first + jnp.arange(rows, dtype=jnp.int32)
    peak = jnp.full((rows, local_heads), -1e30, jnp.float32)
    piece_keys = lax.all_gather(keys, "seq", axis=0, tiled=True)
    piece_values = lax.all_gather(values, "seq", axis=0, tiled=True)
    count = piece_keys.shape[0]
    score = (
        jnp.einsum("qhd,khd->qhk", query, piece_keys, preferred_element_type=jnp.float32) * factor
    )
    key_pos = jnp.arange(count, dtype=jnp.int32)
    allowed = (key_pos[None, :] <= query_pos[:, None]) & (segments[None, :] == own_ids[:, None])
    allowed = allowed[:, None, :]
    masked_scores = jnp.where(allowed, score, -1e30)
    new_peak = jnp.maximum(peak, jnp.max(masked_scores, axis=2))
    weight = jnp.where(allowed, jnp.exp(score - new_peak[:, :, None]), 0.0)
    mass = jnp.sum(weight, axis=2)
    accum = jnp.einsum(
        "qhk,khd->qhd",
        weight.astype(jnp.bfloat16),
        piece_values,
        preferred_element_type=jnp.float32,
    )
    peak, mass, accum = (new_peak, mass, accum)
    context = (accum / mass[:, :, None]).reshape(rows, local_heads * DH).astype(jnp.bfloat16)
    return (hidden, context)


def turn_tables(count):
    turns = (2 * np.arange(count)[:, None] + 1) * np.arange(count)[None, :] % (4 * count)
    angle = np.pi * turns / (2 * count)
    table = np.concatenate([np.cos(angle), np.sin(angle)], axis=0)
    high = table.astype(ml_dtypes.bfloat16)
    low = (table - high.astype(np.float64)).astype(ml_dtypes.bfloat16)
    return high, low


def bf_dot(left, right):
    return jnp.dot(left, right, preferred_element_type=jnp.float32)


def aligned(
    branches,
    residual,
    segments,
    long_filter,
    short_taps,
    skip_gain,
    out_weight,
    norm_gain,
    head_weight,
):
    rows = branches.shape[0]
    channels = branches.shape[2]
    shards = lax.axis_size("seq")
    rank = lax.axis_index("seq")
    first = rank * rows
    own = channels // shards
    count = rows * shards
    stacked = jnp.concatenate(
        [jnp.swapaxes(branches, 0, 1), long_filter.astype(jnp.bfloat16)[None]], axis=0
    )
    whole = lax.all_to_all(stacked, "seq", split_axis=2, concat_axis=1, tiled=True)
    slots = jnp.swapaxes(head_weight, 0, 1)
    taps = lax.dynamic_slice_in_dim(short_taps, rank * own, own, axis=2)
    gain = lax.dynamic_slice_in_dim(skip_gain, rank * own, own)
    inputs = whole[:3].astype(jnp.float32)
    featured = taps[:, 0, :][:, None, :] * inputs
    for offset in (1, 2):
        earlier = jnp.pad(inputs, ((0, 0), (offset, 0), (0, 0)))[:, :count]
        before = jnp.pad(segments, (offset, 0), constant_values=-1)[:count]
        same = (before == segments)[None, :, None]
        featured = featured + jnp.where(same, taps[:, offset, :][:, None, :] * earlier, 0.0)
    mixed = featured[1] * featured[2]
    high, low = turn_tables(count)
    both = jnp.concatenate([mixed.astype(jnp.bfloat16), whole[3]], axis=1)
    spec = bf_dot(high, both) + bf_dot(low, both)
    mix_cos, mix_sin = spec[:count, :own], spec[count:, :own]
    fil_cos, fil_sin = spec[:count, own:], spec[count:, own:]
    product = jnp.concatenate(
        [mix_cos * fil_cos - mix_sin * fil_sin, mix_cos * fil_sin + mix_sin * fil_cos], axis=0
    ).astype(jnp.bfloat16)
    conv = (bf_dot(high.T, product) + bf_dot(low.T, product)) / count
    gated = (featured[0] * (conv + gain * mixed)).astype(jnp.bfloat16)
    gated = lax.all_to_all(gated, "seq", split_axis=0, concat_axis=1, tiled=True)
    mixed_out = bf_dot(lax.all_gather(gated, "tp", axis=1, tiled=True), out_weight)
    hidden = (residual.astype(jnp.float32) + mixed_out).astype(jnp.bfloat16)
    wide = lax.all_gather(hidden, "tp", axis=1, tiled=True).astype(jnp.float32)
    scale = lax.rsqrt(jnp.mean(wide * wide, axis=1, keepdims=True) + EPSILON)
    normed = (wide * scale * norm_gain).astype(jnp.bfloat16)
    query, keys, values = [bf_dot(normed, slots[j]).astype(jnp.bfloat16) for j in range(3)]
    pairs = lax.all_gather(jnp.concatenate([keys, values], axis=1), "seq", axis=0, tiled=True)
    keys, values = pairs[:, :channels], pairs[:, channels:]
    own_ids = lax.dynamic_slice_in_dim(segments, first, rows)
    query_pos = first + jnp.arange(rows, dtype=jnp.int32)
    key_pos = jnp.arange(count, dtype=jnp.int32)
    allowed = (key_pos[None, :] <= query_pos[:, None]) & (segments[None, :] == own_ids[:, None])
    parts = []
    for head in range(channels // DH):
        cols = slice(head * DH, (head + 1) * DH)
        score = jnp.einsum(
            "qd,kd->qk", query[:, cols], keys[:, cols], preferred_element_type=jnp.float32
        ) / math.sqrt(DH)
        score = jnp.where(allowed, score, -1e30)
        weight = jnp.where(allowed, jnp.exp(score - jnp.max(score, axis=1, keepdims=True)), 0.0)
        mass = jnp.sum(weight, axis=1, keepdims=True)
        parts.append(bf_dot(weight.astype(jnp.bfloat16), values[:, cols]) / mass)
    context = jnp.concatenate(parts, axis=1).astype(jnp.bfloat16)
    return (hidden, context)


def solution(mesh):
    placed = (
        P(("groups", "seq"), None, "tp"),
        P(("groups", "seq"), "tp"),
        P("groups"),
        P("seq", "tp"),
        P(None, None, "tp"),
        P("tp"),
        P(None, "tp"),
        P(),
        P(None, None, "tp"),
    )
    def chosen(*arrays):
        channels, rows = arrays[0].shape[2], arrays[0].shape[0]
        shards = lax.axis_size("seq")
        fits = channels % (shards * 128) == 0 and rows % 128 == 0 and shards * rows <= 1024
        return aligned(*arrays) if fits else local(*arrays)

    return jax.shard_map(
        chosen,
        mesh=mesh,
        in_specs=placed,
        out_specs=(P(("groups", "seq"), "tp"), P(("groups", "seq"), "tp")),
        check_vma=False,
    )
```

```python
import functools
import math

import jax
import ml_dtypes
import numpy as np
import jax.numpy as jnp
from jax import lax
from jax.experimental import pallas as pl
from jax.experimental.pallas import tpu as pltpu
from jax.sharding import PartitionSpec as P

DH = 128


EPSILON = 1e-05
HIGHEST = lax.Precision.HIGHEST
TWO_PI = 2.0 * math.pi


def passed_along(array, axis, by):
    count = lax.axis_size(axis)
    pairs = [(i, i + by) for i in range(count) if 0 <= i + by < count]
    return lax.ppermute(array, axis, pairs)


def complex_times(left_real, left_imag, right_real, right_imag):
    return (
        left_real * right_real - left_imag * right_imag,
        left_real * right_imag + left_imag * right_real,
    )


def window_convolve(whole, shards):
    count = whole.shape[1]
    rows = count // shards
    span = 2 * shards
    total = 2 * count
    data = whole.reshape(2, shards, rows, whole.shape[2])
    outer_index = jnp.arange(span, dtype=jnp.int32)
    block_index = jnp.arange(shards, dtype=jnp.int32)
    place_index = jnp.arange(rows, dtype=jnp.int32)
    outer = TWO_PI * (outer_index[:, None] * block_index[None, :] % span).astype(jnp.float32) / span
    outer_cos = jnp.cos(outer)
    outer_sin = jnp.sin(outer)
    first_real = jnp.einsum("ka,sabc->skbc", outer_cos, data, precision=HIGHEST)
    first_imag = -jnp.einsum("ka,sabc->skbc", outer_sin, data, precision=HIGHEST)
    twist = (
        TWO_PI * (outer_index[:, None] * place_index[None, :] % total).astype(jnp.float32) / total
    )
    twist_cos = jnp.cos(twist)[:, :, None]
    twist_sin = jnp.sin(twist)[:, :, None]
    turned_real, turned_imag = complex_times(first_real, first_imag, twist_cos, -twist_sin)
    inner = TWO_PI * (place_index[:, None] * place_index[None, :] % rows).astype(jnp.float32) / rows
    inner_cos = jnp.cos(inner)
    inner_sin = jnp.sin(inner)
    spec_real = jnp.einsum("bq,skbc->skqc", inner_cos, turned_real, precision=HIGHEST) + jnp.einsum(
        "bq,skbc->skqc", inner_sin, turned_imag, precision=HIGHEST
    )
    spec_imag = jnp.einsum("bq,skbc->skqc", inner_cos, turned_imag, precision=HIGHEST) - jnp.einsum(
        "bq,skbc->skqc", inner_sin, turned_real, precision=HIGHEST
    )
    prod_real, prod_imag = complex_times(spec_real[0], spec_imag[0], spec_real[1], spec_imag[1])
    back_real = jnp.einsum("qb,kqc->kbc", inner_cos, prod_real, precision=HIGHEST) - jnp.einsum(
        "qb,kqc->kbc", inner_sin, prod_imag, precision=HIGHEST
    )
    back_imag = jnp.einsum("qb,kqc->kbc", inner_cos, prod_imag, precision=HIGHEST) + jnp.einsum(
        "qb,kqc->kbc", inner_sin, prod_real, precision=HIGHEST
    )
    reverted_real, reverted_imag = complex_times(back_real, back_imag, twist_cos, twist_sin)
    result = jnp.einsum("ka,kbc->abc", outer_cos, reverted_real, precision=HIGHEST) - jnp.einsum(
        "ka,kbc->abc", outer_sin, reverted_imag, precision=HIGHEST
    )
    return (result / total).reshape(count, whole.shape[2])


def local(
    branches,
    residual,
    segments,
    long_filter,
    short_taps,
    skip_gain,
    out_weight,
    norm_gain,
    head_weight,
):
    rows = branches.shape[0]
    channels = branches.shape[2]
    shards = lax.axis_size("seq")
    rank = lax.axis_index("seq")
    first = rank * rows
    prior = passed_along(branches[rows - 2 :], "seq", 1)
    padded = jnp.concatenate([prior, branches], axis=0).astype(jnp.float32)
    flagged_positions = jnp.concatenate([jnp.full((2,), -1, jnp.int32), segments])
    window = lax.dynamic_slice_in_dim(flagged_positions, first, rows + 2)
    own_ids = window[2:]
    featured = jnp.zeros((rows, 3, channels), jnp.float32)
    for offset in range(3):
        earlier = padded[2 - offset : 2 - offset + rows]
        same = window[2 - offset : 2 - offset + rows] == own_ids
        featured = featured + jnp.where(
            same[:, None, None], short_taps[:, offset, :][None] * earlier, 0.0
        )
    mixed = featured[:, 1] * featured[:, 2]
    signals = jnp.stack([mixed, long_filter])
    whole = lax.all_to_all(signals, "seq", split_axis=2, concat_axis=1, tiled=True)
    columns = window_convolve(whole, shards)
    conv = lax.all_to_all(columns, "seq", split_axis=0, concat_axis=1, tiled=True)
    gated = (featured[:, 0] * (conv + skip_gain * mixed)).astype(jnp.bfloat16)
    weight_rows = out_weight
    mixed_out = jnp.dot(
        lax.all_gather(gated, "tp", axis=1, tiled=True),
        weight_rows,
        preferred_element_type=jnp.float32,
    )
    hidden = (residual.astype(jnp.float32) + mixed_out).astype(jnp.bfloat16)
    width = head_weight.shape[0]
    flat_weight = head_weight.reshape(width, -1)
    local_wide = hidden.astype(jnp.float32)
    squares = jnp.sum(local_wide * local_wide, axis=1)
    total_squares = lax.psum(squares, "tp")
    scale = lax.rsqrt(total_squares / width + EPSILON)
    local_width = hidden.shape[1]
    local_gain = lax.dynamic_slice_in_dim(
        norm_gain, lax.axis_index("tp") * local_width, local_width
    )
    normed = (local_wide * scale[:, None] * local_gain).astype(jnp.bfloat16)
    weight_rows = flat_weight
    projected = jnp.dot(
        lax.all_gather(normed, "tp", axis=1, tiled=True),
        weight_rows,
        preferred_element_type=jnp.float32,
    )
    projected = projected.astype(jnp.bfloat16).reshape(rows, 3, -1, DH)
    query = projected[:, 0]
    keys = projected[:, 1]
    values = projected[:, 2]
    local_heads = query.shape[1]
    factor = 1.0 / math.sqrt(DH)
    query_pos = first + jnp.arange(rows, dtype=jnp.int32)
    peak = jnp.full((rows, local_heads), -1e30, jnp.float32)
    piece_keys = lax.all_gather(keys, "seq", axis=0, tiled=True)
    piece_values = lax.all_gather(values, "seq", axis=0, tiled=True)
    count = piece_keys.shape[0]
    score = (
        jnp.einsum("qhd,khd->qhk", query, piece_keys, preferred_element_type=jnp.float32) * factor
    )
    key_pos = jnp.arange(count, dtype=jnp.int32)
    allowed = (key_pos[None, :] <= query_pos[:, None]) & (segments[None, :] == own_ids[:, None])
    allowed = allowed[:, None, :]
    masked_scores = jnp.where(allowed, score, -1e30)
    new_peak = jnp.maximum(peak, jnp.max(masked_scores, axis=2))
    weight = jnp.where(allowed, jnp.exp(score - new_peak[:, :, None]), 0.0)
    mass = jnp.sum(weight, axis=2)
    accum = jnp.einsum(
        "qhk,khd->qhd",
        weight.astype(jnp.bfloat16),
        piece_values,
        preferred_element_type=jnp.float32,
    )
    peak, mass, accum = (new_peak, mass, accum)
    context = (accum / mass[:, :, None]).reshape(rows, local_heads * DH).astype(jnp.bfloat16)
    return (hidden, context)


def turn_tables(count):
    turns = (2 * np.arange(count)[:, None] + 1) * np.arange(count)[None, :] % (4 * count)
    angle = np.pi * turns / (2 * count)
    table = np.concatenate([np.cos(angle), np.sin(angle)], axis=0)
    high = table.astype(ml_dtypes.bfloat16)
    low = (table - high.astype(np.float64)).astype(ml_dtypes.bfloat16)
    return high, low


def bf_dot(left, right):
    return jnp.dot(left, right, preferred_element_type=jnp.float32)


def span(index, size):
    return pl.ds(pl.multiple_of(index * size, size), size)


def remote(src, dst, send, recv, **where):
    return pltpu.make_async_remote_copy(
        src_ref=src,
        dst_ref=dst,
        send_sem=send,
        recv_sem=recv,
        device_id=where,
        device_id_type=pl.DeviceIdType.MESH,
    )


def pair_gather(buf, x, m, wide, send, recv, consume):
    chips = m // 2
    sibling = x + 1 - 2 * lax.rem(x, 2)

    def block(i):
        return buf.at[:, span(i, wide)]

    sent = []

    def ship(i, slot, peer):
        copy = remote(block(i), block(i), send.at[slot], recv.at[slot], tp=peer)
        copy.start()
        sent.append(copy)

    def arrive(i, slot):
        remote(block(i), block(i), send.at[slot], recv.at[slot], tp=sibling).wait_recv()

    for c in range(1, chips):
        ship(x, c, lax.rem(x + 2 * c, m))
    ship(x, 0, sibling)
    consume(x)
    arrive(sibling, 0)
    consume(sibling)
    for c in range(1, chips):
        source = lax.rem(x + m - 2 * c, m)
        arrive(source, c)
        ship(source, chips - 1 + c, sibling)
        consume(source)
    for c in range(1, chips):
        source = lax.rem(sibling + m - 2 * c, m)
        arrive(source, chips - 1 + c)
        consume(source)
    return sent


def layer_kernel(
    n,
    m,
    branches,
    filt,
    residual,
    segs,
    taps,
    skip,
    gain,
    high_in,
    low_in,
    high_t_in,
    low_t_in,
    out_w_in,
    head_in,
    hidden_out,
    context_out,
    fil_stage,
    sig,
    fil,
    high,
    low,
    high_t,
    low_t,
    out_w,
    head,
    seg_wide,
    g_send,
    g_all,
    acc,
    h_all,
    n_all,
    squares,
    kv_acc,
    kv,
    local_sem,
    a_send,
    a_recv,
    f_send,
    f_recv,
    b_send,
    b_recv,
    c_send,
    c_recv,
    d_send,
    d_recv,
    k_send,
    k_recv,
):
    z = lax.axis_index("seq")
    x = lax.axis_index("tp")
    rows, channels = filt.shape
    count, own = fil.shape
    width = h_all.shape[1]
    local_width = residual.shape[1]
    reach = kv.shape[0] - 1
    barrier = pltpu.get_barrier_semaphore()
    for d in range(1, n):
        pl.semaphore_signal(
            barrier, inc=1, device_id={"seq": lax.rem(z + d, n)}, device_id_type=pl.DeviceIdType.MESH
        )
    for d in range(1, m):
        pl.semaphore_signal(
            barrier, inc=1, device_id={"tp": lax.rem(x + d, m)}, device_id_type=pl.DeviceIdType.MESH
        )
    fil_stage[...] = filt[...].astype(jnp.bfloat16)
    pl.semaphore_wait(barrier, n + m - 2)
    sent = []
    for d in range(1, n):
        peer = lax.rem(z + d, n)
        copy = remote(
            branches.at[:, :, span(peer, own)],
            sig.at[:, span(z, rows), :],
            a_send.at[d],
            a_recv.at[d],
            seq=peer,
        )
        copy.start()
        sent.append(copy)
        copy = remote(
            fil_stage.at[:, span(peer, own)],
            fil.at[span(z, rows), :],
            f_send.at[d],
            f_recv.at[d],
            seq=peer,
        )
        copy.start()
        sent.append(copy)
    mine = pltpu.make_async_copy(
        branches.at[:, :, span(z, own)], sig.at[:, span(z, rows), :], local_sem.at[0]
    )
    mine.start()
    loads = []
    for i, (src, dst) in enumerate(
        (
            (high_in, high),
            (low_in, low),
            (high_t_in, high_t),
            (low_t_in, low_t),
            (out_w_in, out_w),
            (head_in.at[1], head.at[1]),
            (head_in.at[2], head.at[2]),
            (head_in.at[0], head.at[0]),
        )
    ):
        load = pltpu.make_async_copy(src, dst, local_sem.at[1 + i])
        load.start()
        loads.append(load)
    fil[span(z, rows), :] = fil_stage[:, span(z, own)]
    for d in range(1, reach + 1):

        @pl.when(z < d)
        def _(d=d):
            kv[d] = jnp.zeros(kv.shape[1:], kv.dtype)

    ids = jnp.broadcast_to(segs[...].astype(jnp.float32), (own, count)).T
    seg_wide[...] = ids
    place = lax.broadcasted_iota(jnp.int32, (count, own), 0)
    same = [
        (pltpu.roll(ids, offset, 0) == ids) & (place >= offset) for offset in (1, 2)
    ]
    mine.wait()
    for d in range(1, n):
        peer = lax.rem(z + n - d, n)
        remote(
            branches.at[:, :, span(peer, own)],
            sig.at[:, span(peer, rows), :],
            a_send.at[d],
            a_recv.at[d],
            seq=peer,
        ).wait_recv()
        remote(
            fil_stage.at[:, span(peer, own)],
            fil.at[span(peer, rows), :],
            f_send.at[d],
            f_recv.at[d],
            seq=peer,
        ).wait_recv()
    featured = []
    for j in range(3):
        wide = sig[j].astype(jnp.float32)
        total = taps[j, pl.ds(0, 1), span(z, own)] * wide
        for offset in (1, 2):
            term = taps[j, pl.ds(offset, 1), span(z, own)] * pltpu.roll(wide, offset, 0)
            total = total + jnp.where(same[offset - 1], term, 0.0)
        featured.append(total)
    mixed = featured[1] * featured[2]
    for load in loads[:4]:
        load.wait()
    both = jnp.concatenate([mixed.astype(jnp.bfloat16), fil[...]], axis=1)
    spec = bf_dot(high[...], both) + bf_dot(low[...], both)
    mix_cos, mix_sin = spec[:count, :own], spec[count:, :own]
    fil_cos, fil_sin = spec[:count, own:], spec[count:, own:]
    product = jnp.concatenate(
        [mix_cos * fil_cos - mix_sin * fil_sin, mix_cos * fil_sin + mix_sin * fil_cos], axis=0
    ).astype(jnp.bfloat16)
    conv = (bf_dot(high_t[...], product) + bf_dot(low_t[...], product)) * (1.0 / count)
    gated = featured[0] * (conv + skip[:, span(z, own)] * mixed)
    g_send[...] = gated.astype(jnp.bfloat16)

    def column(shard):
        return g_all.at[:, span(x * n + shard, own)]

    for d in range(1, n):
        peer = lax.rem(z + d, n)
        copy = remote(
            g_send.at[span(peer, rows), :], column(z), b_send.at[d], b_recv.at[d], seq=peer
        )
        copy.start()
        sent.append(copy)
    g_all[:, span(x * n + z, own)] = g_send[span(z, rows), :]
    acc[...] = residual[...].astype(jnp.float32)
    loads[4].wait()
    for d in range(1, n):
        peer = lax.rem(z + n - d, n)
        remote(
            g_send.at[span(peer, rows), :], column(peer), b_send.at[d], b_recv.at[d], seq=peer
        ).wait_recv()

    def out_part(i):
        acc[...] += bf_dot(g_all[:, span(i, channels)], out_w[span(i, channels), :])

    sent += pair_gather(g_all, x, m, channels, c_send, c_recv, out_part)
    hidden = acc[...].astype(jnp.bfloat16)
    hidden_out[...] = hidden
    h_all[:, span(x, local_width)] = hidden
    squares[...] = jnp.zeros_like(squares)
    kv_acc[...] = jnp.zeros_like(kv_acc)
    loads[5].wait()
    loads[6].wait()

    def head_part(i):
        block = h_all[:, span(i, local_width)].astype(jnp.float32)
        squares[...] += jnp.sum(block * block, axis=1, keepdims=True)
        scaled = (block * gain[:, span(i, local_width)]).astype(jnp.bfloat16)
        n_all[:, span(i, local_width)] = scaled
        for j in (1, 2):
            kv_acc[j - 1] += bf_dot(scaled, head[j, span(i, local_width), :])

    sent += pair_gather(h_all, x, m, local_width, d_send, d_recv, head_part)
    scale = lax.rsqrt(squares[:, :1] * (1.0 / width) + EPSILON)
    for j in range(2):
        kv[0, j] = (kv_acc[j] * scale).astype(jnp.bfloat16)

    def kv_copy(d, peer):
        return remote(kv.at[0], kv.at[d], k_send.at[d], k_recv.at[d], seq=peer)

    for d in range(1, reach + 1):

        @pl.when(z + d < n)
        def _(d=d):
            kv_copy(d, z + d).start()

    loads[7].wait()
    query = (bf_dot(n_all[...], head[0]) * scale).astype(jnp.bfloat16)
    own_ids = seg_wide[span(z, rows), :][:, :1]
    query_pos = z * rows + lax.broadcasted_iota(jnp.int32, (rows, rows), 0)
    allowed = []
    for d in range(reach + 1):
        shard = lax.max(z - d, 0)
        key_pos = (z - d) * rows + lax.broadcasted_iota(jnp.int32, (rows, rows), 1)
        ids = segs[:, span(shard, rows)].astype(jnp.float32)
        allowed.append((key_pos >= 0) & (key_pos <= query_pos) & (ids == own_ids))
    allowed = jnp.concatenate(allowed, axis=1)
    for d in range(1, reach + 1):

        @pl.when(z >= d)
        def _(d=d):
            kv_copy(d, z - d).wait_recv()

    for h in range(channels // DH):
        cols = slice(h * DH, (h + 1) * DH)
        keys = jnp.concatenate([kv[d, 0, :, cols] for d in range(reach + 1)], axis=0)
        values = jnp.concatenate([kv[d, 1, :, cols] for d in range(reach + 1)], axis=0)
        score = lax.dot_general(
            query[:, cols], keys, (((1,), (1,)), ((), ())), preferred_element_type=jnp.float32
        ) * (1.0 / math.sqrt(DH))
        score = jnp.where(allowed, score, -1e30)
        weight = jnp.where(allowed, jnp.exp(score - jnp.max(score, axis=1, keepdims=True)), 0.0)
        mass = jnp.sum(weight, axis=1, keepdims=True)
        part = bf_dot(weight.astype(jnp.bfloat16), values) / mass
        context_out[:, cols] = part.astype(jnp.bfloat16)
    for copy in sent:
        copy.wait_send()
    for d in range(1, reach + 1):

        @pl.when(z + d < n)
        def _(d=d):
            kv_copy(d, z + d).wait_send()


def aligned(
    branches,
    residual,
    segments,
    long_filter,
    short_taps,
    skip_gain,
    out_weight,
    norm_gain,
    head_weight,
):
    rows, _, channels = branches.shape
    local_width = residual.shape[1]
    n = lax.axis_size("seq")
    m = lax.axis_size("tp")
    own = channels // n
    count = rows * n
    width = head_weight.shape[0]
    reach = n // 2
    high, low = turn_tables(count)
    vmem = pl.BlockSpec(memory_space=pltpu.VMEM)
    hbm = pl.BlockSpec(memory_space=pl.ANY)
    bf16, f32 = jnp.bfloat16, jnp.float32
    dma = pltpu.SemaphoreType.DMA
    return pl.pallas_call(
        functools.partial(layer_kernel, n, m),
        out_shape=(
            jax.ShapeDtypeStruct((rows, local_width), bf16),
            jax.ShapeDtypeStruct((rows, channels), bf16),
        ),
        in_specs=[hbm] + [vmem] * 6 + [hbm] * 6,
        out_specs=(vmem, vmem),
        scratch_shapes=[
            pltpu.VMEM((rows, channels), bf16),
            pltpu.VMEM((3, count, own), bf16),
            pltpu.VMEM((count, own), bf16),
            pltpu.VMEM((2 * count, count), bf16),
            pltpu.VMEM((2 * count, count), bf16),
            pltpu.VMEM((count, 2 * count), bf16),
            pltpu.VMEM((count, 2 * count), bf16),
            pltpu.VMEM(out_weight.shape, bf16),
            pltpu.VMEM((3, width, channels), bf16),
            pltpu.VMEM((count, own), f32),
            pltpu.VMEM((count, own), bf16),
            pltpu.VMEM((rows, m * channels), bf16),
            pltpu.VMEM((rows, local_width), f32),
            pltpu.VMEM((rows, width), bf16),
            pltpu.VMEM((rows, width), bf16),
            pltpu.VMEM((rows, 128), f32),
            pltpu.VMEM((2, rows, channels), f32),
            pltpu.VMEM((reach + 1, 2, rows, channels), bf16),
            dma((9,)),
            dma((n,)),
            dma((n,)),
            dma((n,)),
            dma((n,)),
            dma((n,)),
            dma((n,)),
            dma((m,)),
            dma((m,)),
            dma((m,)),
            dma((m,)),
            dma((reach + 1,)),
            dma((reach + 1,)),
        ],
        compiler_params=pltpu.CompilerParams(
            collective_id=0, has_side_effects=True, vmem_limit_bytes=50 * 2**20
        ),
    )(
        jnp.swapaxes(branches, 0, 1),
        long_filter,
        residual,
        segments.reshape(1, -1),
        short_taps,
        skip_gain.reshape(1, -1),
        norm_gain.reshape(1, -1),
        high,
        low,
        np.ascontiguousarray(high.T),
        np.ascontiguousarray(low.T),
        out_weight,
        jnp.swapaxes(head_weight, 0, 1),
    )


def solution(mesh):
    placed = (
        P(("groups", "seq"), None, "tp"),
        P(("groups", "seq"), "tp"),
        P("groups"),
        P("seq", "tp"),
        P(None, None, "tp"),
        P("tp"),
        P(None, "tp"),
        P(),
        P(None, None, "tp"),
    )
    def chosen(*arrays):
        channels, rows = arrays[0].shape[2], arrays[0].shape[0]
        shards = lax.axis_size("seq")
        fits = channels % (shards * 128) == 0 and rows % 128 == 0 and shards * rows <= 1024
        fits = fits and shards % 2 == 0 and lax.axis_size("tp") % 2 == 0
        return aligned(*arrays) if fits else local(*arrays)

    return jax.shard_map(
        chosen,
        mesh=mesh,
        in_specs=placed,
        out_specs=(P(("groups", "seq"), "tp"), P(("groups", "seq"), "tp")),
        check_vma=False,
    )
```

```python
import functools
import math

import jax
import ml_dtypes
import numpy as np
import jax.numpy as jnp
from jax import lax
from jax.experimental import pallas as pl
from jax.experimental.pallas import tpu as pltpu
from jax.sharding import PartitionSpec as P

DH = 128


EPSILON = 1e-05
HIGHEST = lax.Precision.HIGHEST
TWO_PI = 2.0 * math.pi


def passed_along(array, axis, by):
    count = lax.axis_size(axis)
    pairs = [(i, i + by) for i in range(count) if 0 <= i + by < count]
    return lax.ppermute(array, axis, pairs)


def complex_times(left_real, left_imag, right_real, right_imag):
    return (
        left_real * right_real - left_imag * right_imag,
        left_real * right_imag + left_imag * right_real,
    )


def window_convolve(whole, shards):
    count = whole.shape[1]
    rows = count // shards
    span = 2 * shards
    total = 2 * count
    data = whole.reshape(2, shards, rows, whole.shape[2])
    outer_index = jnp.arange(span, dtype=jnp.int32)
    block_index = jnp.arange(shards, dtype=jnp.int32)
    place_index = jnp.arange(rows, dtype=jnp.int32)
    outer = TWO_PI * (outer_index[:, None] * block_index[None, :] % span).astype(jnp.float32) / span
    outer_cos = jnp.cos(outer)
    outer_sin = jnp.sin(outer)
    first_real = jnp.einsum("ka,sabc->skbc", outer_cos, data, precision=HIGHEST)
    first_imag = -jnp.einsum("ka,sabc->skbc", outer_sin, data, precision=HIGHEST)
    twist = (
        TWO_PI * (outer_index[:, None] * place_index[None, :] % total).astype(jnp.float32) / total
    )
    twist_cos = jnp.cos(twist)[:, :, None]
    twist_sin = jnp.sin(twist)[:, :, None]
    turned_real, turned_imag = complex_times(first_real, first_imag, twist_cos, -twist_sin)
    inner = TWO_PI * (place_index[:, None] * place_index[None, :] % rows).astype(jnp.float32) / rows
    inner_cos = jnp.cos(inner)
    inner_sin = jnp.sin(inner)
    spec_real = jnp.einsum("bq,skbc->skqc", inner_cos, turned_real, precision=HIGHEST) + jnp.einsum(
        "bq,skbc->skqc", inner_sin, turned_imag, precision=HIGHEST
    )
    spec_imag = jnp.einsum("bq,skbc->skqc", inner_cos, turned_imag, precision=HIGHEST) - jnp.einsum(
        "bq,skbc->skqc", inner_sin, turned_real, precision=HIGHEST
    )
    prod_real, prod_imag = complex_times(spec_real[0], spec_imag[0], spec_real[1], spec_imag[1])
    back_real = jnp.einsum("qb,kqc->kbc", inner_cos, prod_real, precision=HIGHEST) - jnp.einsum(
        "qb,kqc->kbc", inner_sin, prod_imag, precision=HIGHEST
    )
    back_imag = jnp.einsum("qb,kqc->kbc", inner_cos, prod_imag, precision=HIGHEST) + jnp.einsum(
        "qb,kqc->kbc", inner_sin, prod_real, precision=HIGHEST
    )
    reverted_real, reverted_imag = complex_times(back_real, back_imag, twist_cos, twist_sin)
    result = jnp.einsum("ka,kbc->abc", outer_cos, reverted_real, precision=HIGHEST) - jnp.einsum(
        "ka,kbc->abc", outer_sin, reverted_imag, precision=HIGHEST
    )
    return (result / total).reshape(count, whole.shape[2])


def local(
    branches,
    residual,
    segments,
    long_filter,
    short_taps,
    skip_gain,
    out_weight,
    norm_gain,
    head_weight,
):
    rows = branches.shape[0]
    channels = branches.shape[2]
    shards = lax.axis_size("seq")
    rank = lax.axis_index("seq")
    first = rank * rows
    prior = passed_along(branches[rows - 2 :], "seq", 1)
    padded = jnp.concatenate([prior, branches], axis=0).astype(jnp.float32)
    flagged_positions = jnp.concatenate([jnp.full((2,), -1, jnp.int32), segments])
    window = lax.dynamic_slice_in_dim(flagged_positions, first, rows + 2)
    own_ids = window[2:]
    featured = jnp.zeros((rows, 3, channels), jnp.float32)
    for offset in range(3):
        earlier = padded[2 - offset : 2 - offset + rows]
        same = window[2 - offset : 2 - offset + rows] == own_ids
        featured = featured + jnp.where(
            same[:, None, None], short_taps[:, offset, :][None] * earlier, 0.0
        )
    mixed = featured[:, 1] * featured[:, 2]
    signals = jnp.stack([mixed, long_filter])
    whole = lax.all_to_all(signals, "seq", split_axis=2, concat_axis=1, tiled=True)
    columns = window_convolve(whole, shards)
    conv = lax.all_to_all(columns, "seq", split_axis=0, concat_axis=1, tiled=True)
    gated = (featured[:, 0] * (conv + skip_gain * mixed)).astype(jnp.bfloat16)
    weight_rows = out_weight
    mixed_out = jnp.dot(
        lax.all_gather(gated, "tp", axis=1, tiled=True),
        weight_rows,
        preferred_element_type=jnp.float32,
    )
    hidden = (residual.astype(jnp.float32) + mixed_out).astype(jnp.bfloat16)
    width = head_weight.shape[0]
    flat_weight = head_weight.reshape(width, -1)
    local_wide = hidden.astype(jnp.float32)
    squares = jnp.sum(local_wide * local_wide, axis=1)
    total_squares = lax.psum(squares, "tp")
    scale = lax.rsqrt(total_squares / width + EPSILON)
    local_width = hidden.shape[1]
    local_gain = lax.dynamic_slice_in_dim(
        norm_gain, lax.axis_index("tp") * local_width, local_width
    )
    normed = (local_wide * scale[:, None] * local_gain).astype(jnp.bfloat16)
    weight_rows = flat_weight
    projected = jnp.dot(
        lax.all_gather(normed, "tp", axis=1, tiled=True),
        weight_rows,
        preferred_element_type=jnp.float32,
    )
    projected = projected.astype(jnp.bfloat16).reshape(rows, 3, -1, DH)
    query = projected[:, 0]
    keys = projected[:, 1]
    values = projected[:, 2]
    local_heads = query.shape[1]
    factor = 1.0 / math.sqrt(DH)
    query_pos = first + jnp.arange(rows, dtype=jnp.int32)
    peak = jnp.full((rows, local_heads), -1e30, jnp.float32)
    piece_keys = lax.all_gather(keys, "seq", axis=0, tiled=True)
    piece_values = lax.all_gather(values, "seq", axis=0, tiled=True)
    count = piece_keys.shape[0]
    score = (
        jnp.einsum("qhd,khd->qhk", query, piece_keys, preferred_element_type=jnp.float32) * factor
    )
    key_pos = jnp.arange(count, dtype=jnp.int32)
    allowed = (key_pos[None, :] <= query_pos[:, None]) & (segments[None, :] == own_ids[:, None])
    allowed = allowed[:, None, :]
    masked_scores = jnp.where(allowed, score, -1e30)
    new_peak = jnp.maximum(peak, jnp.max(masked_scores, axis=2))
    weight = jnp.where(allowed, jnp.exp(score - new_peak[:, :, None]), 0.0)
    mass = jnp.sum(weight, axis=2)
    accum = jnp.einsum(
        "qhk,khd->qhd",
        weight.astype(jnp.bfloat16),
        piece_values,
        preferred_element_type=jnp.float32,
    )
    peak, mass, accum = (new_peak, mass, accum)
    context = (accum / mass[:, :, None]).reshape(rows, local_heads * DH).astype(jnp.bfloat16)
    return (hidden, context)


def turn_tables(count):
    turns = (2 * np.arange(count)[:, None] + 1) * np.arange(count)[None, :] % (4 * count)
    angle = np.pi * turns / (2 * count)
    table = np.concatenate([np.cos(angle), np.sin(angle)], axis=0)
    high = table.astype(ml_dtypes.bfloat16)
    low = (table - high.astype(np.float64)).astype(ml_dtypes.bfloat16)
    return high, low


def bf_dot(left, right):
    return jnp.dot(left, right, preferred_element_type=jnp.float32)


def span(index, size):
    return pl.ds(pl.multiple_of(index * size, size), size)


def remote(src, dst, send, recv, **where):
    return pltpu.make_async_remote_copy(
        src_ref=src,
        dst_ref=dst,
        send_sem=send,
        recv_sem=recv,
        device_id=where,
        device_id_type=pl.DeviceIdType.MESH,
    )


def pair_gather(buf, x, m, wide, send, recv, consume):
    chips = m // 2
    sibling = x + 1 - 2 * lax.rem(x, 2)

    def block(i):
        return buf.at[:, span(i, wide)]

    sent = []

    def ship(i, slot, peer):
        copy = remote(block(i), block(i), send.at[slot], recv.at[slot], tp=peer)
        copy.start()
        sent.append(copy)

    def arrive(i, slot):
        remote(block(i), block(i), send.at[slot], recv.at[slot], tp=sibling).wait_recv()

    for c in range(1, chips):
        ship(x, c, lax.rem(x + 2 * c, m))
    ship(x, 0, sibling)
    consume(x)
    arrive(sibling, 0)
    consume(sibling)
    for c in range(1, chips):
        source = lax.rem(x + m - 2 * c, m)
        arrive(source, c)
        ship(source, chips - 1 + c, sibling)
        consume(source)
    for c in range(1, chips):
        source = lax.rem(sibling + m - 2 * c, m)
        arrive(source, chips - 1 + c)
        consume(source)
    return sent


def layer_kernel(
    n,
    m,
    branches,
    filt_in,
    residual_in,
    segs_in,
    taps_in,
    skip_in,
    gain_in,
    high_in,
    low_in,
    high_t_in,
    low_t_in,
    out_w_in,
    head_in,
    hidden_out,
    context_out,
    filt,
    residual,
    segs,
    taps,
    skip,
    gain,
    ctx,
    fil_stage,
    sig,
    fil,
    high,
    low,
    high_t,
    low_t,
    out_w,
    head,
    seg_wide,
    g_send,
    g_all,
    acc,
    h_all,
    n_all,
    squares,
    kv_acc,
    kv,
    local_sem,
    a_send,
    a_recv,
    f_send,
    f_recv,
    b_send,
    b_recv,
    c_send,
    c_recv,
    d_send,
    d_recv,
    k_send,
    k_recv,
):
    z = lax.axis_index("seq")
    x = lax.axis_index("tp")
    rows, channels = filt.shape
    count, own = fil.shape
    width = h_all.shape[1]
    local_width = residual.shape[1]
    reach = kv.shape[0] - 1
    barrier = pltpu.get_barrier_semaphore()
    for d in range(1, n):
        pl.semaphore_signal(
            barrier, inc=1, device_id={"seq": lax.rem(z + d, n)}, device_id_type=pl.DeviceIdType.MESH
        )
    for d in range(1, m):
        pl.semaphore_signal(
            barrier, inc=1, device_id={"tp": lax.rem(x + d, m)}, device_id_type=pl.DeviceIdType.MESH
        )
    early = []
    for i, (src, dst) in enumerate(
        (
            (filt_in, filt),
            (segs_in, segs),
            (taps_in, taps),
            (skip_in, skip),
            (residual_in, residual),
            (gain_in, gain),
        )
    ):
        load = pltpu.make_async_copy(src, dst, local_sem.at[9 + i])
        load.start()
        early.append(load)
    pl.semaphore_wait(barrier, n + m - 2)
    sent = []

    def sig_copy(kind, d, peer, source):
        part = pl.ds(1, 2) if kind == 0 else pl.ds(0, 1)
        return remote(
            branches.at[part, :, span(peer, own)],
            sig.at[part, span(source, rows), :],
            a_send.at[kind, d],
            a_recv.at[kind, d],
            seq=peer,
        )

    for d in range(1, n):
        copy = sig_copy(0, d, lax.rem(z + d, n), z)
        copy.start()
        sent.append(copy)
    early[0].wait()
    fil_stage[...] = filt[...].astype(jnp.bfloat16)
    for d in range(1, n):
        peer = lax.rem(z + d, n)
        copy = remote(
            fil_stage.at[:, span(peer, own)],
            fil.at[span(z, rows), :],
            f_send.at[d],
            f_recv.at[d],
            seq=peer,
        )
        copy.start()
        sent.append(copy)
    for d in range(1, n):
        copy = sig_copy(1, d, lax.rem(z + d, n), z)
        copy.start()
        sent.append(copy)
    mine = pltpu.make_async_copy(
        branches.at[:, :, span(z, own)], sig.at[:, span(z, rows), :], local_sem.at[0]
    )
    mine.start()
    loads = []
    for i, (src, dst) in enumerate(
        (
            (high_in, high),
            (low_in, low),
            (high_t_in, high_t),
            (low_t_in, low_t),
            (out_w_in, out_w),
            (head_in.at[1], head.at[1]),
            (head_in.at[2], head.at[2]),
            (head_in.at[0], head.at[0]),
        )
    ):
        load = pltpu.make_async_copy(src, dst, local_sem.at[1 + i])
        load.start()
        loads.append(load)
    fil[span(z, rows), :] = fil_stage[:, span(z, own)]
    for d in range(1, reach + 1):

        @pl.when(z < d)
        def _(d=d):
            kv[d] = jnp.zeros(kv.shape[1:], kv.dtype)

    early[1].wait()
    ids = jnp.broadcast_to(segs[...].astype(jnp.float32), (own, count)).T
    seg_wide[...] = ids
    place = lax.broadcasted_iota(jnp.int32, (count, own), 0)
    same = [
        (pltpu.roll(ids, offset, 0) == ids) & (place >= offset) for offset in (1, 2)
    ]
    mine.wait()
    for d in range(1, n):
        peer = lax.rem(z + n - d, n)
        sig_copy(0, d, peer, peer).wait_recv()
        remote(
            fil_stage.at[:, span(peer, own)],
            fil.at[span(peer, rows), :],
            f_send.at[d],
            f_recv.at[d],
            seq=peer,
        ).wait_recv()
    early[2].wait()

    def feature(j):
        wide = sig[j].astype(jnp.float32)
        total = taps[j, pl.ds(0, 1), span(z, own)] * wide
        for offset in (1, 2):
            term = taps[j, pl.ds(offset, 1), span(z, own)] * pltpu.roll(wide, offset, 0)
            total = total + jnp.where(same[offset - 1], term, 0.0)
        return total

    mixed = feature(1) * feature(2)
    for load in loads[:4]:
        load.wait()
    both = jnp.concatenate([mixed.astype(jnp.bfloat16), fil[...]], axis=1)
    spec = bf_dot(high[...], both) + bf_dot(low[...], both)
    mix_cos, mix_sin = spec[:count, :own], spec[count:, :own]
    fil_cos, fil_sin = spec[:count, own:], spec[count:, own:]
    product = jnp.concatenate(
        [mix_cos * fil_cos - mix_sin * fil_sin, mix_cos * fil_sin + mix_sin * fil_cos], axis=0
    ).astype(jnp.bfloat16)
    conv = (bf_dot(high_t[...], product) + bf_dot(low_t[...], product)) * (1.0 / count)
    early[3].wait()
    for d in range(1, n):
        peer = lax.rem(z + n - d, n)
        sig_copy(1, d, peer, peer).wait_recv()
    gated = feature(0) * (conv + skip[:, span(z, own)] * mixed)
    g_send[...] = gated.astype(jnp.bfloat16)

    def column(shard):
        return g_all.at[:, span(x * n + shard, own)]

    for d in range(1, n):
        peer = lax.rem(z + d, n)
        copy = remote(
            g_send.at[span(peer, rows), :], column(z), b_send.at[d], b_recv.at[d], seq=peer
        )
        copy.start()
        sent.append(copy)
    g_all[:, span(x * n + z, own)] = g_send[span(z, rows), :]
    early[4].wait()
    acc[...] = residual[...].astype(jnp.float32)
    loads[4].wait()
    for d in range(1, n):
        peer = lax.rem(z + n - d, n)
        remote(
            g_send.at[span(peer, rows), :], column(peer), b_send.at[d], b_recv.at[d], seq=peer
        ).wait_recv()

    def out_part(i):
        acc[...] += bf_dot(g_all[:, span(i, channels)], out_w[span(i, channels), :])

    sent += pair_gather(g_all, x, m, channels, c_send, c_recv, out_part)
    hidden = acc[...].astype(jnp.bfloat16)
    h_all[:, span(x, local_width)] = hidden
    written = [
        pltpu.make_async_copy(h_all.at[:, span(x, local_width)], hidden_out, local_sem.at[15])
    ]
    written[0].start()
    early[5].wait()
    squares[...] = jnp.zeros_like(squares)
    kv_acc[...] = jnp.zeros_like(kv_acc)
    loads[5].wait()
    loads[6].wait()

    def head_part(i):
        block = h_all[:, span(i, local_width)].astype(jnp.float32)
        squares[...] += jnp.sum(block * block, axis=1, keepdims=True)
        scaled = (block * gain[:, span(i, local_width)]).astype(jnp.bfloat16)
        n_all[:, span(i, local_width)] = scaled
        for j in (1, 2):
            kv_acc[j - 1] += bf_dot(scaled, head[j, span(i, local_width), :])

    sent += pair_gather(h_all, x, m, local_width, d_send, d_recv, head_part)
    scale = lax.rsqrt(squares[:, :1] * (1.0 / width) + EPSILON)
    for j in range(2):
        kv[0, j] = (kv_acc[j] * scale).astype(jnp.bfloat16)

    def kv_copy(d, part):
        return remote(
            kv.at[d - 1, part],
            kv.at[d, part],
            k_send.at[d, part],
            k_recv.at[d, part],
            seq=lax.rem(z + 1, n),
        )

    for part in range(2):

        @pl.when(z + 1 < n)
        def _(part=part):
            kv_copy(1, part).start()

    loads[7].wait()
    query = (bf_dot(n_all[...], head[0]) * scale).astype(jnp.bfloat16)
    own_ids = seg_wide[span(z, rows), :][:, :1]
    query_pos = z * rows + lax.broadcasted_iota(jnp.int32, (rows, rows), 0)
    allowed = []
    for d in range(reach + 1):
        shard = lax.max(z - d, 0)
        key_pos = (z - d) * rows + lax.broadcasted_iota(jnp.int32, (rows, rows), 1)
        ids = segs[:, span(shard, rows)].astype(jnp.float32)
        allowed.append((key_pos >= 0) & (key_pos <= query_pos) & (ids == own_ids))
    allowed = jnp.concatenate(allowed, axis=1)
    for d in range(1, reach + 1):
        for part in range(2):

            @pl.when(z >= d)
            def _(d=d, part=part):
                kv_copy(d, part).wait_recv()

            if d < reach:

                @pl.when(jnp.logical_and(z >= d, z + 1 < n))
                def _(d=d, part=part):
                    kv_copy(d + 1, part).start()

    for h in range(channels // DH):
        cols = slice(h * DH, (h + 1) * DH)
        keys = jnp.concatenate([kv[d, 0, :, cols] for d in range(reach + 1)], axis=0)
        values = jnp.concatenate([kv[d, 1, :, cols] for d in range(reach + 1)], axis=0)
        score = lax.dot_general(
            query[:, cols], keys, (((1,), (1,)), ((), ())), preferred_element_type=jnp.float32
        ) * (1.0 / math.sqrt(DH))
        score = jnp.where(allowed, score, -1e30)
        weight = jnp.where(allowed, jnp.exp(score - jnp.max(score, axis=1, keepdims=True)), 0.0)
        mass = jnp.sum(weight, axis=1, keepdims=True)
        part = bf_dot(weight.astype(jnp.bfloat16), values) / mass
        ctx[:, cols] = part.astype(jnp.bfloat16)
    written.append(pltpu.make_async_copy(ctx, context_out, local_sem.at[0]))
    written[1].start()
    for copy in sent:
        copy.wait_send()
    for d in range(1, reach + 1):
        for part in range(2):

            @pl.when(jnp.logical_and(z >= d - 1, z + 1 < n))
            def _(d=d, part=part):
                kv_copy(d, part).wait_send()

    for copy in written:
        copy.wait()


def aligned(
    branches,
    residual,
    segments,
    long_filter,
    short_taps,
    skip_gain,
    out_weight,
    norm_gain,
    head_weight,
):
    rows, _, channels = branches.shape
    local_width = residual.shape[1]
    n = lax.axis_size("seq")
    m = lax.axis_size("tp")
    own = channels // n
    count = rows * n
    width = head_weight.shape[0]
    reach = n // 2
    high, low = turn_tables(count)
    hbm = pl.BlockSpec(memory_space=pltpu.HBM)
    bf16, f32 = jnp.bfloat16, jnp.float32
    dma = pltpu.SemaphoreType.DMA
    return pl.pallas_call(
        functools.partial(layer_kernel, n, m),
        out_shape=(
            jax.ShapeDtypeStruct((rows, local_width), bf16),
            jax.ShapeDtypeStruct((rows, channels), bf16),
        ),
        in_specs=[hbm] * 13,
        out_specs=(hbm, hbm),
        scratch_shapes=[
            pltpu.VMEM((rows, channels), f32),
            pltpu.VMEM((rows, local_width), bf16),
            pltpu.VMEM((1, count), jnp.int32),
            pltpu.VMEM(short_taps.shape, f32),
            pltpu.VMEM((1, channels), f32),
            pltpu.VMEM((1, width), f32),
            pltpu.VMEM((rows, channels), bf16),
            pltpu.VMEM((rows, channels), bf16),
            pltpu.VMEM((3, count, own), bf16),
            pltpu.VMEM((count, own), bf16),
            pltpu.VMEM((2 * count, count), bf16),
            pltpu.VMEM((2 * count, count), bf16),
            pltpu.VMEM((count, 2 * count), bf16),
            pltpu.VMEM((count, 2 * count), bf16),
            pltpu.VMEM(out_weight.shape, bf16),
            pltpu.VMEM((3, width, channels), bf16),
            pltpu.VMEM((count, own), f32),
            pltpu.VMEM((count, own), bf16),
            pltpu.VMEM((rows, m * channels), bf16),
            pltpu.VMEM((rows, local_width), f32),
            pltpu.VMEM((rows, width), bf16),
            pltpu.VMEM((rows, width), bf16),
            pltpu.VMEM((rows, 128), f32),
            pltpu.VMEM((2, rows, channels), f32),
            pltpu.VMEM((reach + 1, 2, rows, channels), bf16),
            dma((16,)),
            dma((2, n)),
            dma((2, n)),
            dma((n,)),
            dma((n,)),
            dma((n,)),
            dma((n,)),
            dma((m,)),
            dma((m,)),
            dma((m,)),
            dma((m,)),
            dma((reach + 1, 2)),
            dma((reach + 1, 2)),
        ],
        compiler_params=pltpu.CompilerParams(
            collective_id=0, has_side_effects=True, vmem_limit_bytes=62 * 2**20
        ),
    )(
        jnp.swapaxes(branches, 0, 1),
        long_filter,
        residual,
        segments.reshape(1, -1),
        short_taps,
        skip_gain.reshape(1, -1),
        norm_gain.reshape(1, -1),
        high,
        low,
        np.ascontiguousarray(high.T),
        np.ascontiguousarray(low.T),
        out_weight,
        jnp.swapaxes(head_weight, 0, 1),
    )


def solution(mesh):
    placed = (
        P(("groups", "seq"), None, "tp"),
        P(("groups", "seq"), "tp"),
        P("groups"),
        P("seq", "tp"),
        P(None, None, "tp"),
        P("tp"),
        P(None, "tp"),
        P(),
        P(None, None, "tp"),
    )
    def chosen(*arrays):
        channels, rows = arrays[0].shape[2], arrays[0].shape[0]
        shards = lax.axis_size("seq")
        fits = channels % (shards * 128) == 0 and rows % 128 == 0 and shards * rows <= 1024
        fits = fits and shards % 2 == 0 and lax.axis_size("tp") % 2 == 0
        return aligned(*arrays) if fits else local(*arrays)

    return jax.shard_map(
        chosen,
        mesh=mesh,
        in_specs=placed,
        out_specs=(P(("groups", "seq"), "tp"), P(("groups", "seq"), "tp")),
        check_vma=False,
    )
```

```python
import functools
import math

import jax
import ml_dtypes
import numpy as np
import jax.numpy as jnp
from jax import lax
from jax.experimental import pallas as pl
from jax.experimental.pallas import tpu as pltpu
from jax.sharding import PartitionSpec as P

DH = 128


EPSILON = 1e-05
HIGHEST = lax.Precision.HIGHEST
TWO_PI = 2.0 * math.pi


def passed_along(array, axis, by):
    count = lax.axis_size(axis)
    pairs = [(i, i + by) for i in range(count) if 0 <= i + by < count]
    return lax.ppermute(array, axis, pairs)


def complex_times(left_real, left_imag, right_real, right_imag):
    return (
        left_real * right_real - left_imag * right_imag,
        left_real * right_imag + left_imag * right_real,
    )


def window_convolve(whole, shards):
    count = whole.shape[1]
    rows = count // shards
    span = 2 * shards
    total = 2 * count
    data = whole.reshape(2, shards, rows, whole.shape[2])
    outer_index = jnp.arange(span, dtype=jnp.int32)
    block_index = jnp.arange(shards, dtype=jnp.int32)
    place_index = jnp.arange(rows, dtype=jnp.int32)
    outer = TWO_PI * (outer_index[:, None] * block_index[None, :] % span).astype(jnp.float32) / span
    outer_cos = jnp.cos(outer)
    outer_sin = jnp.sin(outer)
    first_real = jnp.einsum("ka,sabc->skbc", outer_cos, data, precision=HIGHEST)
    first_imag = -jnp.einsum("ka,sabc->skbc", outer_sin, data, precision=HIGHEST)
    twist = (
        TWO_PI * (outer_index[:, None] * place_index[None, :] % total).astype(jnp.float32) / total
    )
    twist_cos = jnp.cos(twist)[:, :, None]
    twist_sin = jnp.sin(twist)[:, :, None]
    turned_real, turned_imag = complex_times(first_real, first_imag, twist_cos, -twist_sin)
    inner = TWO_PI * (place_index[:, None] * place_index[None, :] % rows).astype(jnp.float32) / rows
    inner_cos = jnp.cos(inner)
    inner_sin = jnp.sin(inner)
    spec_real = jnp.einsum("bq,skbc->skqc", inner_cos, turned_real, precision=HIGHEST) + jnp.einsum(
        "bq,skbc->skqc", inner_sin, turned_imag, precision=HIGHEST
    )
    spec_imag = jnp.einsum("bq,skbc->skqc", inner_cos, turned_imag, precision=HIGHEST) - jnp.einsum(
        "bq,skbc->skqc", inner_sin, turned_real, precision=HIGHEST
    )
    prod_real, prod_imag = complex_times(spec_real[0], spec_imag[0], spec_real[1], spec_imag[1])
    back_real = jnp.einsum("qb,kqc->kbc", inner_cos, prod_real, precision=HIGHEST) - jnp.einsum(
        "qb,kqc->kbc", inner_sin, prod_imag, precision=HIGHEST
    )
    back_imag = jnp.einsum("qb,kqc->kbc", inner_cos, prod_imag, precision=HIGHEST) + jnp.einsum(
        "qb,kqc->kbc", inner_sin, prod_real, precision=HIGHEST
    )
    reverted_real, reverted_imag = complex_times(back_real, back_imag, twist_cos, twist_sin)
    result = jnp.einsum("ka,kbc->abc", outer_cos, reverted_real, precision=HIGHEST) - jnp.einsum(
        "ka,kbc->abc", outer_sin, reverted_imag, precision=HIGHEST
    )
    return (result / total).reshape(count, whole.shape[2])


def local(
    branches,
    residual,
    segments,
    long_filter,
    short_taps,
    skip_gain,
    out_weight,
    norm_gain,
    head_weight,
):
    rows = branches.shape[0]
    channels = branches.shape[2]
    shards = lax.axis_size("seq")
    rank = lax.axis_index("seq")
    first = rank * rows
    prior = passed_along(branches[rows - 2 :], "seq", 1)
    padded = jnp.concatenate([prior, branches], axis=0).astype(jnp.float32)
    flagged_positions = jnp.concatenate([jnp.full((2,), -1, jnp.int32), segments])
    window = lax.dynamic_slice_in_dim(flagged_positions, first, rows + 2)
    own_ids = window[2:]
    featured = jnp.zeros((rows, 3, channels), jnp.float32)
    for offset in range(3):
        earlier = padded[2 - offset : 2 - offset + rows]
        same = window[2 - offset : 2 - offset + rows] == own_ids
        featured = featured + jnp.where(
            same[:, None, None], short_taps[:, offset, :][None] * earlier, 0.0
        )
    mixed = featured[:, 1] * featured[:, 2]
    signals = jnp.stack([mixed, long_filter])
    whole = lax.all_to_all(signals, "seq", split_axis=2, concat_axis=1, tiled=True)
    columns = window_convolve(whole, shards)
    conv = lax.all_to_all(columns, "seq", split_axis=0, concat_axis=1, tiled=True)
    gated = (featured[:, 0] * (conv + skip_gain * mixed)).astype(jnp.bfloat16)
    weight_rows = out_weight
    mixed_out = jnp.dot(
        lax.all_gather(gated, "tp", axis=1, tiled=True),
        weight_rows,
        preferred_element_type=jnp.float32,
    )
    hidden = (residual.astype(jnp.float32) + mixed_out).astype(jnp.bfloat16)
    width = head_weight.shape[0]
    flat_weight = head_weight.reshape(width, -1)
    local_wide = hidden.astype(jnp.float32)
    squares = jnp.sum(local_wide * local_wide, axis=1)
    total_squares = lax.psum(squares, "tp")
    scale = lax.rsqrt(total_squares / width + EPSILON)
    local_width = hidden.shape[1]
    local_gain = lax.dynamic_slice_in_dim(
        norm_gain, lax.axis_index("tp") * local_width, local_width
    )
    normed = (local_wide * scale[:, None] * local_gain).astype(jnp.bfloat16)
    weight_rows = flat_weight
    projected = jnp.dot(
        lax.all_gather(normed, "tp", axis=1, tiled=True),
        weight_rows,
        preferred_element_type=jnp.float32,
    )
    projected = projected.astype(jnp.bfloat16).reshape(rows, 3, -1, DH)
    query = projected[:, 0]
    keys = projected[:, 1]
    values = projected[:, 2]
    local_heads = query.shape[1]
    factor = 1.0 / math.sqrt(DH)
    query_pos = first + jnp.arange(rows, dtype=jnp.int32)
    peak = jnp.full((rows, local_heads), -1e30, jnp.float32)
    piece_keys = lax.all_gather(keys, "seq", axis=0, tiled=True)
    piece_values = lax.all_gather(values, "seq", axis=0, tiled=True)
    count = piece_keys.shape[0]
    score = (
        jnp.einsum("qhd,khd->qhk", query, piece_keys, preferred_element_type=jnp.float32) * factor
    )
    key_pos = jnp.arange(count, dtype=jnp.int32)
    allowed = (key_pos[None, :] <= query_pos[:, None]) & (segments[None, :] == own_ids[:, None])
    allowed = allowed[:, None, :]
    masked_scores = jnp.where(allowed, score, -1e30)
    new_peak = jnp.maximum(peak, jnp.max(masked_scores, axis=2))
    weight = jnp.where(allowed, jnp.exp(score - new_peak[:, :, None]), 0.0)
    mass = jnp.sum(weight, axis=2)
    accum = jnp.einsum(
        "qhk,khd->qhd",
        weight.astype(jnp.bfloat16),
        piece_values,
        preferred_element_type=jnp.float32,
    )
    peak, mass, accum = (new_peak, mass, accum)
    context = (accum / mass[:, :, None]).reshape(rows, local_heads * DH).astype(jnp.bfloat16)
    return (hidden, context)


def turn_tables(count):
    turns = (2 * np.arange(count)[:, None] + 1) * np.arange(count)[None, :] % (4 * count)
    angle = np.pi * turns / (2 * count)
    table = np.concatenate([np.cos(angle), np.sin(angle)], axis=0)
    high = table.astype(ml_dtypes.bfloat16)
    low = (table - high.astype(np.float64)).astype(ml_dtypes.bfloat16)
    return high, low


def bf_dot(left, right):
    return jnp.dot(left, right, preferred_element_type=jnp.float32)


def span(index, size):
    return pl.ds(pl.multiple_of(index * size, size), size)


def remote(src, dst, send, recv, **where):
    return pltpu.make_async_remote_copy(
        src_ref=src,
        dst_ref=dst,
        send_sem=send,
        recv_sem=recv,
        device_id=where,
        device_id_type=pl.DeviceIdType.MESH,
    )


def pair_gather(buf, x, m, wide, parts, send, recv, consume):
    chips = m // 2
    sibling = x + 1 - 2 * lax.rem(x, 2)

    def block(i, p):
        return buf.at[:, span(i * parts + p, wide // parts)]

    sent = []

    def ship(i, p, slot, peer):
        copy = remote(block(i, p), block(i, p), send.at[slot, p], recv.at[slot, p], tp=peer)
        copy.start()
        sent.append(copy)

    def arrive(i, p, slot):
        remote(
            block(i, p), block(i, p), send.at[slot, p], recv.at[slot, p], tp=sibling
        ).wait_recv()

    for c in range(1, chips):
        for p in range(parts):
            ship(x, p, c, lax.rem(x + 2 * c, m))
    for p in range(parts):
        ship(x, p, 0, sibling)
    for p in range(parts):
        consume(x * parts + p)
    for p in range(parts):
        arrive(sibling, p, 0)
        consume(sibling * parts + p)
    for c in range(1, chips):
        near = lax.rem(x + m - 2 * c, m)
        far = lax.rem(sibling + m - 2 * c, m)
        for p in range(parts):
            arrive(near, p, c)
            ship(near, p, chips - 1 + c, sibling)
            consume(near * parts + p)
            if p > 0:
                arrive(far, p - 1, chips - 1 + c)
                consume(far * parts + p - 1)
        arrive(far, parts - 1, chips - 1 + c)
        consume(far * parts + parts - 1)
    return sent


def layer_kernel(
    n,
    m,
    branches,
    filt_in,
    residual_in,
    segs_in,
    taps_in,
    skip_in,
    gain_in,
    high_in,
    low_in,
    high_t_in,
    low_t_in,
    out_w_in,
    head_in,
    hidden_out,
    context_out,
    filt,
    residual,
    segs,
    taps,
    skip,
    gain,
    ctx,
    fil_stage,
    sig,
    fil,
    high,
    low,
    high_t,
    low_t,
    out_w,
    head,
    seg_wide,
    g_send,
    g_all,
    acc,
    h_all,
    n_all,
    squares,
    kv_acc,
    kv,
    local_sem,
    a_send,
    a_recv,
    f_send,
    f_recv,
    b_send,
    b_recv,
    c_send,
    c_recv,
    d_send,
    d_recv,
    k_send,
    k_recv,
):
    z = lax.axis_index("seq")
    x = lax.axis_index("tp")
    rows, channels = filt.shape
    count, own = fil.shape
    width = h_all.shape[1]
    local_width = residual.shape[1]
    reach = kv.shape[0] - 1
    barrier = pltpu.get_barrier_semaphore()
    for d in range(1, n):
        pl.semaphore_signal(
            barrier, inc=1, device_id={"seq": lax.rem(z + d, n)}, device_id_type=pl.DeviceIdType.MESH
        )
    for d in range(1, m):
        pl.semaphore_signal(
            barrier, inc=1, device_id={"tp": lax.rem(x + d, m)}, device_id_type=pl.DeviceIdType.MESH
        )
    early = []
    for i, (src, dst) in enumerate(
        (
            (filt_in, filt),
            (segs_in, segs),
            (taps_in, taps),
            (skip_in, skip),
            (residual_in, residual),
            (gain_in, gain),
        )
    ):
        load = pltpu.make_async_copy(src, dst, local_sem.at[9 + i])
        load.start()
        early.append(load)
    pl.semaphore_wait(barrier, n + m - 2)
    sent = []

    def sig_copy(kind, d, peer, source):
        part = pl.ds(1, 2) if kind == 0 else pl.ds(0, 1)
        return remote(
            branches.at[part, :, span(peer, own)],
            sig.at[part, span(source, rows), :],
            a_send.at[kind, d],
            a_recv.at[kind, d],
            seq=peer,
        )

    for d in range(1, n):
        copy = sig_copy(0, d, lax.rem(z + d, n), z)
        copy.start()
        sent.append(copy)
    early[0].wait()
    fil_stage[...] = filt[...].astype(jnp.bfloat16)
    for d in range(1, n):
        peer = lax.rem(z + d, n)
        copy = remote(
            fil_stage.at[:, span(peer, own)],
            fil.at[span(z, rows), :],
            f_send.at[d],
            f_recv.at[d],
            seq=peer,
        )
        copy.start()
        sent.append(copy)
    for d in range(1, n):
        copy = sig_copy(1, d, lax.rem(z + d, n), z)
        copy.start()
        sent.append(copy)
    mine = pltpu.make_async_copy(
        branches.at[:, :, span(z, own)], sig.at[:, span(z, rows), :], local_sem.at[0]
    )
    mine.start()
    loads = []
    for i, (src, dst) in enumerate(
        (
            (high_in, high),
            (low_in, low),
            (high_t_in, high_t),
            (low_t_in, low_t),
            (out_w_in, out_w),
            (head_in.at[1], head.at[1]),
            (head_in.at[2], head.at[2]),
            (head_in.at[0], head.at[0]),
        )
    ):
        load = pltpu.make_async_copy(src, dst, local_sem.at[1 + i])
        load.start()
        loads.append(load)
    fil[span(z, rows), :] = fil_stage[:, span(z, own)]
    for d in range(1, reach + 1):

        @pl.when(z < d)
        def _(d=d):
            kv[d] = jnp.zeros(kv.shape[1:], kv.dtype)

    early[1].wait()
    ids = jnp.broadcast_to(segs[...].astype(jnp.float32), (own, count)).T
    seg_wide[...] = ids
    place = lax.broadcasted_iota(jnp.int32, (count, own), 0)
    same = [
        (pltpu.roll(ids, offset, 0) == ids) & (place >= offset) for offset in (1, 2)
    ]
    mine.wait()
    for d in range(1, n):
        peer = lax.rem(z + n - d, n)
        sig_copy(0, d, peer, peer).wait_recv()
        remote(
            fil_stage.at[:, span(peer, own)],
            fil.at[span(peer, rows), :],
            f_send.at[d],
            f_recv.at[d],
            seq=peer,
        ).wait_recv()
    early[2].wait()

    def feature(j):
        wide = sig[j].astype(jnp.float32)
        total = taps[j, pl.ds(0, 1), span(z, own)] * wide
        for offset in (1, 2):
            term = taps[j, pl.ds(offset, 1), span(z, own)] * pltpu.roll(wide, offset, 0)
            total = total + jnp.where(same[offset - 1], term, 0.0)
        return total

    mixed = feature(1) * feature(2)
    for load in loads[:4]:
        load.wait()
    both = jnp.concatenate([mixed.astype(jnp.bfloat16), fil[...]], axis=1)
    spec = bf_dot(high[...], both) + bf_dot(low[...], both)
    mix_cos, mix_sin = spec[:count, :own], spec[count:, :own]
    fil_cos, fil_sin = spec[:count, own:], spec[count:, own:]
    product = jnp.concatenate(
        [mix_cos * fil_cos - mix_sin * fil_sin, mix_cos * fil_sin + mix_sin * fil_cos], axis=0
    ).astype(jnp.bfloat16)
    conv = (bf_dot(high_t[...], product) + bf_dot(low_t[...], product)) * (1.0 / count)
    early[3].wait()
    for d in range(1, n):
        peer = lax.rem(z + n - d, n)
        sig_copy(1, d, peer, peer).wait_recv()
    gated = feature(0) * (conv + skip[:, span(z, own)] * mixed)
    g_send[...] = gated.astype(jnp.bfloat16)

    def column(shard):
        return g_all.at[:, span(x * n + shard, own)]

    for d in range(1, n):
        peer = lax.rem(z + d, n)
        copy = remote(
            g_send.at[span(peer, rows), :], column(z), b_send.at[d], b_recv.at[d], seq=peer
        )
        copy.start()
        sent.append(copy)
    g_all[:, span(x * n + z, own)] = g_send[span(z, rows), :]
    early[4].wait()
    acc[...] = residual[...].astype(jnp.float32)
    loads[4].wait()
    for d in range(1, n):
        peer = lax.rem(z + n - d, n)
        remote(
            g_send.at[span(peer, rows), :], column(peer), b_send.at[d], b_recv.at[d], seq=peer
        ).wait_recv()

    out_parts, head_parts = c_send.shape[1], d_send.shape[1]
    out_step, head_step = channels // out_parts, local_width // head_parts

    def out_part(i):
        acc[...] += bf_dot(g_all[:, span(i, out_step)], out_w[span(i, out_step), :])

    sent += pair_gather(g_all, x, m, channels, out_parts, c_send, c_recv, out_part)
    hidden = acc[...].astype(jnp.bfloat16)
    h_all[:, span(x, local_width)] = hidden
    written = [
        pltpu.make_async_copy(h_all.at[:, span(x, local_width)], hidden_out, local_sem.at[15])
    ]
    written[0].start()
    early[5].wait()
    squares[...] = jnp.zeros_like(squares)
    kv_acc[...] = jnp.zeros_like(kv_acc)
    loads[5].wait()
    loads[6].wait()

    def head_part(i):
        block = h_all[:, span(i, head_step)].astype(jnp.float32)
        squares[...] += jnp.sum(block * block, axis=1, keepdims=True)
        scaled = (block * gain[:, span(i, head_step)]).astype(jnp.bfloat16)
        n_all[:, span(i, head_step)] = scaled
        for j in (1, 2):
            kv_acc[j - 1] += bf_dot(scaled, head[j, span(i, head_step), :])

    sent += pair_gather(h_all, x, m, local_width, head_parts, d_send, d_recv, head_part)
    scale = lax.rsqrt(squares[:, :1] * (1.0 / width) + EPSILON)
    for j in range(2):
        kv[0, j] = (kv_acc[j] * scale).astype(jnp.bfloat16)

    def kv_copy(d, part):
        return remote(
            kv.at[d - 1, part],
            kv.at[d, part],
            k_send.at[d, part],
            k_recv.at[d, part],
            seq=lax.rem(z + 1, n),
        )

    for part in range(2):

        @pl.when(z + 1 < n)
        def _(part=part):
            kv_copy(1, part).start()

    loads[7].wait()
    query = (bf_dot(n_all[...], head[0]) * scale).astype(jnp.bfloat16)
    own_ids = seg_wide[span(z, rows), :][:, :1]
    query_pos = z * rows + lax.broadcasted_iota(jnp.int32, (rows, rows), 0)
    allowed = []
    for d in range(reach + 1):
        shard = lax.max(z - d, 0)
        key_pos = (z - d) * rows + lax.broadcasted_iota(jnp.int32, (rows, rows), 1)
        ids = segs[:, span(shard, rows)].astype(jnp.float32)
        allowed.append((key_pos >= 0) & (key_pos <= query_pos) & (ids == own_ids))
    allowed = jnp.concatenate(allowed, axis=1)
    heads = [slice(h * DH, (h + 1) * DH) for h in range(channels // DH)]

    def scores(d):
        return [
            lax.dot_general(
                query[:, cols],
                kv[d, 0, :, cols],
                (((1,), (1,)), ((), ())),
                preferred_element_type=jnp.float32,
            )
            for cols in heads
        ]

    def receive(d, part):
        @pl.when(z >= d)
        def _():
            kv_copy(d, part).wait_recv()

        if d < reach:

            @pl.when(jnp.logical_and(z >= d, z + 1 < n))
            def _():
                kv_copy(d + 1, part).start()

    found = [scores(0)]
    for d in range(1, reach + 1):
        receive(d, 0)
        found.append(scores(d))
        if d < reach:
            receive(d, 1)
    weights = []
    for h in range(len(heads)):
        score = jnp.concatenate([block[h] for block in found], axis=1)
        score = jnp.where(allowed, score * (1.0 / math.sqrt(DH)), -1e30)
        weight = jnp.where(allowed, jnp.exp(score - jnp.max(score, axis=1, keepdims=True)), 0.0)
        mass = jnp.sum(weight, axis=1, keepdims=True)
        weights.append((weight.astype(jnp.bfloat16), mass))
    receive(reach, 1)
    for (weight, mass), cols in zip(weights, heads):
        values = jnp.concatenate([kv[d, 1, :, cols] for d in range(reach + 1)], axis=0)
        ctx[:, cols] = (bf_dot(weight, values) / mass).astype(jnp.bfloat16)
    written.append(pltpu.make_async_copy(ctx, context_out, local_sem.at[0]))
    written[1].start()
    for copy in sent:
        copy.wait_send()
    for d in range(1, reach + 1):
        for part in range(2):

            @pl.when(jnp.logical_and(z >= d - 1, z + 1 < n))
            def _(d=d, part=part):
                kv_copy(d, part).wait_send()

    for copy in written:
        copy.wait()


def aligned(
    branches,
    residual,
    segments,
    long_filter,
    short_taps,
    skip_gain,
    out_weight,
    norm_gain,
    head_weight,
):
    rows, _, channels = branches.shape
    local_width = residual.shape[1]
    n = lax.axis_size("seq")
    m = lax.axis_size("tp")
    own = channels // n
    count = rows * n
    width = head_weight.shape[0]
    reach = n // 2
    high, low = turn_tables(count)
    hbm = pl.BlockSpec(memory_space=pltpu.HBM)
    bf16, f32 = jnp.bfloat16, jnp.float32
    dma = pltpu.SemaphoreType.DMA
    return pl.pallas_call(
        functools.partial(layer_kernel, n, m),
        out_shape=(
            jax.ShapeDtypeStruct((rows, local_width), bf16),
            jax.ShapeDtypeStruct((rows, channels), bf16),
        ),
        in_specs=[hbm] * 13,
        out_specs=(hbm, hbm),
        scratch_shapes=[
            pltpu.VMEM((rows, channels), f32),
            pltpu.VMEM((rows, local_width), bf16),
            pltpu.VMEM((1, count), jnp.int32),
            pltpu.VMEM(short_taps.shape, f32),
            pltpu.VMEM((1, channels), f32),
            pltpu.VMEM((1, width), f32),
            pltpu.VMEM((rows, channels), bf16),
            pltpu.VMEM((rows, channels), bf16),
            pltpu.VMEM((3, count, own), bf16),
            pltpu.VMEM((count, own), bf16),
            pltpu.VMEM((2 * count, count), bf16),
            pltpu.VMEM((2 * count, count), bf16),
            pltpu.VMEM((count, 2 * count), bf16),
            pltpu.VMEM((count, 2 * count), bf16),
            pltpu.VMEM(out_weight.shape, bf16),
            pltpu.VMEM((3, width, channels), bf16),
            pltpu.VMEM((count, own), f32),
            pltpu.VMEM((count, own), bf16),
            pltpu.VMEM((rows, m * channels), bf16),
            pltpu.VMEM((rows, local_width), f32),
            pltpu.VMEM((rows, width), bf16),
            pltpu.VMEM((rows, width), bf16),
            pltpu.VMEM((rows, 128), f32),
            pltpu.VMEM((2, rows, channels), f32),
            pltpu.VMEM((reach + 1, 2, rows, channels), bf16),
            dma((16,)),
            dma((2, n)),
            dma((2, n)),
            dma((n,)),
            dma((n,)),
            dma((n,)),
            dma((n,)),
            dma((m, 2)),
            dma((m, 2)),
            dma((m, 4)),
            dma((m, 4)),
            dma((reach + 1, 2)),
            dma((reach + 1, 2)),
        ],
        compiler_params=pltpu.CompilerParams(
            collective_id=0, has_side_effects=True, vmem_limit_bytes=62 * 2**20
        ),
    )(
        jnp.swapaxes(branches, 0, 1),
        long_filter,
        residual,
        segments.reshape(1, -1),
        short_taps,
        skip_gain.reshape(1, -1),
        norm_gain.reshape(1, -1),
        high,
        low,
        np.ascontiguousarray(high.T),
        np.ascontiguousarray(low.T),
        out_weight,
        jnp.swapaxes(head_weight, 0, 1),
    )


def solution(mesh):
    placed = (
        P(("groups", "seq"), None, "tp"),
        P(("groups", "seq"), "tp"),
        P("groups"),
        P("seq", "tp"),
        P(None, None, "tp"),
        P("tp"),
        P(None, "tp"),
        P(),
        P(None, None, "tp"),
    )
    def chosen(*arrays):
        channels, rows = arrays[0].shape[2], arrays[0].shape[0]
        shards = lax.axis_size("seq")
        fits = channels % (shards * 128) == 0 and arrays[1].shape[1] % 512 == 0 and rows % 128 == 0 and shards * rows <= 1024
        fits = fits and shards % 2 == 0 and lax.axis_size("tp") % 2 == 0
        return aligned(*arrays) if fits else local(*arrays)

    return jax.shard_map(
        chosen,
        mesh=mesh,
        in_specs=placed,
        out_specs=(P(("groups", "seq"), "tp"), P(("groups", "seq"), "tp")),
        check_vma=False,
    )
```

```python
import functools
import math

import jax
import ml_dtypes
import numpy as np
import jax.numpy as jnp
from jax import lax
from jax.experimental import pallas as pl
from jax.experimental.pallas import tpu as pltpu
from jax.sharding import PartitionSpec as P

DH = 128


EPSILON = 1e-05
HIGHEST = lax.Precision.HIGHEST
TWO_PI = 2.0 * math.pi


def passed_along(array, axis, by):
    count = lax.axis_size(axis)
    pairs = [(i, i + by) for i in range(count) if 0 <= i + by < count]
    return lax.ppermute(array, axis, pairs)


def complex_times(left_real, left_imag, right_real, right_imag):
    return (
        left_real * right_real - left_imag * right_imag,
        left_real * right_imag + left_imag * right_real,
    )


def window_convolve(whole, shards):
    count = whole.shape[1]
    rows = count // shards
    span = 2 * shards
    total = 2 * count
    data = whole.reshape(2, shards, rows, whole.shape[2])
    outer_index = jnp.arange(span, dtype=jnp.int32)
    block_index = jnp.arange(shards, dtype=jnp.int32)
    place_index = jnp.arange(rows, dtype=jnp.int32)
    outer = TWO_PI * (outer_index[:, None] * block_index[None, :] % span).astype(jnp.float32) / span
    outer_cos = jnp.cos(outer)
    outer_sin = jnp.sin(outer)
    first_real = jnp.einsum("ka,sabc->skbc", outer_cos, data, precision=HIGHEST)
    first_imag = -jnp.einsum("ka,sabc->skbc", outer_sin, data, precision=HIGHEST)
    twist = (
        TWO_PI * (outer_index[:, None] * place_index[None, :] % total).astype(jnp.float32) / total
    )
    twist_cos = jnp.cos(twist)[:, :, None]
    twist_sin = jnp.sin(twist)[:, :, None]
    turned_real, turned_imag = complex_times(first_real, first_imag, twist_cos, -twist_sin)
    inner = TWO_PI * (place_index[:, None] * place_index[None, :] % rows).astype(jnp.float32) / rows
    inner_cos = jnp.cos(inner)
    inner_sin = jnp.sin(inner)
    spec_real = jnp.einsum("bq,skbc->skqc", inner_cos, turned_real, precision=HIGHEST) + jnp.einsum(
        "bq,skbc->skqc", inner_sin, turned_imag, precision=HIGHEST
    )
    spec_imag = jnp.einsum("bq,skbc->skqc", inner_cos, turned_imag, precision=HIGHEST) - jnp.einsum(
        "bq,skbc->skqc", inner_sin, turned_real, precision=HIGHEST
    )
    prod_real, prod_imag = complex_times(spec_real[0], spec_imag[0], spec_real[1], spec_imag[1])
    back_real = jnp.einsum("qb,kqc->kbc", inner_cos, prod_real, precision=HIGHEST) - jnp.einsum(
        "qb,kqc->kbc", inner_sin, prod_imag, precision=HIGHEST
    )
    back_imag = jnp.einsum("qb,kqc->kbc", inner_cos, prod_imag, precision=HIGHEST) + jnp.einsum(
        "qb,kqc->kbc", inner_sin, prod_real, precision=HIGHEST
    )
    reverted_real, reverted_imag = complex_times(back_real, back_imag, twist_cos, twist_sin)
    result = jnp.einsum("ka,kbc->abc", outer_cos, reverted_real, precision=HIGHEST) - jnp.einsum(
        "ka,kbc->abc", outer_sin, reverted_imag, precision=HIGHEST
    )
    return (result / total).reshape(count, whole.shape[2])


def local(
    branches,
    residual,
    segments,
    long_filter,
    short_taps,
    skip_gain,
    out_weight,
    norm_gain,
    head_weight,
):
    rows = branches.shape[0]
    channels = branches.shape[2]
    shards = lax.axis_size("seq")
    rank = lax.axis_index("seq")
    first = rank * rows
    prior = passed_along(branches[rows - 2 :], "seq", 1)
    padded = jnp.concatenate([prior, branches], axis=0).astype(jnp.float32)
    flagged_positions = jnp.concatenate([jnp.full((2,), -1, jnp.int32), segments])
    window = lax.dynamic_slice_in_dim(flagged_positions, first, rows + 2)
    own_ids = window[2:]
    featured = jnp.zeros((rows, 3, channels), jnp.float32)
    for offset in range(3):
        earlier = padded[2 - offset : 2 - offset + rows]
        same = window[2 - offset : 2 - offset + rows] == own_ids
        featured = featured + jnp.where(
            same[:, None, None], short_taps[:, offset, :][None] * earlier, 0.0
        )
    mixed = featured[:, 1] * featured[:, 2]
    signals = jnp.stack([mixed, long_filter])
    whole = lax.all_to_all(signals, "seq", split_axis=2, concat_axis=1, tiled=True)
    columns = window_convolve(whole, shards)
    conv = lax.all_to_all(columns, "seq", split_axis=0, concat_axis=1, tiled=True)
    gated = (featured[:, 0] * (conv + skip_gain * mixed)).astype(jnp.bfloat16)
    weight_rows = out_weight
    mixed_out = jnp.dot(
        lax.all_gather(gated, "tp", axis=1, tiled=True),
        weight_rows,
        preferred_element_type=jnp.float32,
    )
    hidden = (residual.astype(jnp.float32) + mixed_out).astype(jnp.bfloat16)
    width = head_weight.shape[0]
    flat_weight = head_weight.reshape(width, -1)
    local_wide = hidden.astype(jnp.float32)
    squares = jnp.sum(local_wide * local_wide, axis=1)
    total_squares = lax.psum(squares, "tp")
    scale = lax.rsqrt(total_squares / width + EPSILON)
    local_width = hidden.shape[1]
    local_gain = lax.dynamic_slice_in_dim(
        norm_gain, lax.axis_index("tp") * local_width, local_width
    )
    normed = (local_wide * scale[:, None] * local_gain).astype(jnp.bfloat16)
    weight_rows = flat_weight
    projected = jnp.dot(
        lax.all_gather(normed, "tp", axis=1, tiled=True),
        weight_rows,
        preferred_element_type=jnp.float32,
    )
    projected = projected.astype(jnp.bfloat16).reshape(rows, 3, -1, DH)
    query = projected[:, 0]
    keys = projected[:, 1]
    values = projected[:, 2]
    local_heads = query.shape[1]
    factor = 1.0 / math.sqrt(DH)
    query_pos = first + jnp.arange(rows, dtype=jnp.int32)
    peak = jnp.full((rows, local_heads), -1e30, jnp.float32)
    piece_keys = lax.all_gather(keys, "seq", axis=0, tiled=True)
    piece_values = lax.all_gather(values, "seq", axis=0, tiled=True)
    count = piece_keys.shape[0]
    score = (
        jnp.einsum("qhd,khd->qhk", query, piece_keys, preferred_element_type=jnp.float32) * factor
    )
    key_pos = jnp.arange(count, dtype=jnp.int32)
    allowed = (key_pos[None, :] <= query_pos[:, None]) & (segments[None, :] == own_ids[:, None])
    allowed = allowed[:, None, :]
    masked_scores = jnp.where(allowed, score, -1e30)
    new_peak = jnp.maximum(peak, jnp.max(masked_scores, axis=2))
    weight = jnp.where(allowed, jnp.exp(score - new_peak[:, :, None]), 0.0)
    mass = jnp.sum(weight, axis=2)
    accum = jnp.einsum(
        "qhk,khd->qhd",
        weight.astype(jnp.bfloat16),
        piece_values,
        preferred_element_type=jnp.float32,
    )
    peak, mass, accum = (new_peak, mass, accum)
    context = (accum / mass[:, :, None]).reshape(rows, local_heads * DH).astype(jnp.bfloat16)
    return (hidden, context)


def turn_tables(count):
    turns = (2 * np.arange(count)[:, None] + 1) * np.arange(count)[None, :] % (4 * count)
    angle = np.pi * turns / (2 * count)
    table = np.concatenate([np.cos(angle), np.sin(angle)], axis=0)
    high = table.astype(ml_dtypes.bfloat16)
    low = (table - high.astype(np.float64)).astype(ml_dtypes.bfloat16)
    return high, low


def bf_dot(left, right):
    return jnp.dot(left, right, preferred_element_type=jnp.float32)


def span(index, size):
    return pl.ds(pl.multiple_of(index * size, size), size)


def remote(src, dst, send, recv, **where):
    return pltpu.make_async_remote_copy(
        src_ref=src,
        dst_ref=dst,
        send_sem=send,
        recv_sem=recv,
        device_id=where,
        device_id_type=pl.DeviceIdType.MESH,
    )


def pair_gather(buf, x, m, wide, parts, send, recv, consume):
    chips = m // 2
    sibling = x + 1 - 2 * lax.rem(x, 2)

    def block(i, p):
        return buf.at[:, span(i * parts + p, wide // parts)]

    sent = []

    def ship(i, p, slot, peer):
        copy = remote(block(i, p), block(i, p), send.at[slot, p], recv.at[slot, p], tp=peer)
        copy.start()
        sent.append(copy)

    def arrive(i, p, slot):
        remote(
            block(i, p), block(i, p), send.at[slot, p], recv.at[slot, p], tp=sibling
        ).wait_recv()

    for c in range(1, chips):
        for p in range(parts):
            ship(x, p, c, lax.rem(x + 2 * c, m))
    for p in range(parts):
        ship(x, p, 0, sibling)
    for p in range(parts):
        consume(x * parts + p)
    for p in range(parts):
        arrive(sibling, p, 0)
        consume(sibling * parts + p)
    for c in range(1, chips):
        near = lax.rem(x + m - 2 * c, m)
        far = lax.rem(sibling + m - 2 * c, m)
        for p in range(parts):
            arrive(near, p, c)
            ship(near, p, chips - 1 + c, sibling)
            consume(near * parts + p)
            if p > 0:
                arrive(far, p - 1, chips - 1 + c)
                consume(far * parts + p - 1)
        arrive(far, parts - 1, chips - 1 + c)
        consume(far * parts + parts - 1)
    return sent


def layer_kernel(
    n,
    m,
    branches,
    filt_in,
    residual_in,
    segs_in,
    taps_in,
    skip_in,
    gain_in,
    high_in,
    low_in,
    high_t_in,
    low_t_in,
    out_w_in,
    head_in,
    hidden_out,
    context_out,
    filt,
    residual,
    segs,
    taps,
    skip,
    gain,
    ctx,
    fil_stage,
    sig,
    fil,
    high,
    low,
    high_t,
    low_t,
    out_w,
    head,
    seg_wide,
    g_send,
    g_all,
    acc,
    h_all,
    n_all,
    squares,
    kv_acc,
    kv,
    local_sem,
    a_send,
    a_recv,
    f_send,
    f_recv,
    b_send,
    b_recv,
    c_send,
    c_recv,
    d_send,
    d_recv,
    k_send,
    k_recv,
):
    z = lax.axis_index("seq")
    x = lax.axis_index("tp")
    rows, channels = filt.shape
    count, own = fil.shape
    width = h_all.shape[1]
    local_width = residual.shape[1]
    reach = kv.shape[0] - 1
    barrier = pltpu.get_barrier_semaphore()
    for d in range(1, n):
        pl.semaphore_signal(
            barrier, inc=1, device_id={"seq": lax.rem(z + d, n)}, device_id_type=pl.DeviceIdType.MESH
        )
    for d in range(1, m):
        pl.semaphore_signal(
            barrier, inc=1, device_id={"tp": lax.rem(x + d, m)}, device_id_type=pl.DeviceIdType.MESH
        )
    early = []
    for i, (src, dst) in enumerate(
        (
            (filt_in, filt),
            (segs_in, segs),
            (taps_in, taps),
            (skip_in, skip),
            (residual_in, residual),
            (gain_in, gain),
        )
    ):
        load = pltpu.make_async_copy(src, dst, local_sem.at[9 + i])
        load.start()
        early.append(load)
    pl.semaphore_wait(barrier, n + m - 2)
    sent = []

    def sig_copy(kind, d, peer, source):
        part = pl.ds(1, 2) if kind == 0 else pl.ds(0, 1)
        return remote(
            branches.at[part, :, span(peer, own)],
            sig.at[part, span(source, rows), :],
            a_send.at[kind, d],
            a_recv.at[kind, d],
            seq=peer,
        )

    for d in range(1, n):
        copy = sig_copy(0, d, lax.rem(z + d, n), z)
        copy.start()
        sent.append(copy)
    early[0].wait()
    fil_stage[...] = filt[...].astype(jnp.bfloat16)
    for d in range(1, n):
        peer = lax.rem(z + d, n)
        copy = remote(
            fil_stage.at[:, span(peer, own)],
            fil.at[span(z, rows), :],
            f_send.at[d],
            f_recv.at[d],
            seq=peer,
        )
        copy.start()
        sent.append(copy)
    for d in range(1, n):
        copy = sig_copy(1, d, lax.rem(z + d, n), z)
        copy.start()
        sent.append(copy)
    mine = pltpu.make_async_copy(
        branches.at[:, :, span(z, own)], sig.at[:, span(z, rows), :], local_sem.at[0]
    )
    mine.start()
    loads = []
    for i, (src, dst) in enumerate(
        (
            (high_in, high),
            (low_in, low),
            (high_t_in, high_t),
            (low_t_in, low_t),
            (out_w_in, out_w),
            (head_in.at[1], head.at[1]),
            (head_in.at[2], head.at[2]),
            (head_in.at[0], head.at[0]),
        )
    ):
        load = pltpu.make_async_copy(src, dst, local_sem.at[1 + i])
        load.start()
        loads.append(load)
    fil[span(z, rows), :] = fil_stage[:, span(z, own)]
    for d in range(1, reach + 1):

        @pl.when(z < d)
        def _(d=d):
            kv[d] = jnp.zeros(kv.shape[1:], kv.dtype)

    early[1].wait()
    ids = jnp.broadcast_to(segs[...].astype(jnp.float32), (own, count)).T
    seg_wide[...] = ids
    place = lax.broadcasted_iota(jnp.int32, (count, own), 0)
    same = [
        (pltpu.roll(ids, offset, 0) == ids) & (place >= offset) for offset in (1, 2)
    ]
    mine.wait()
    for d in range(1, n):
        peer = lax.rem(z + n - d, n)
        sig_copy(0, d, peer, peer).wait_recv()
        remote(
            fil_stage.at[:, span(peer, own)],
            fil.at[span(peer, rows), :],
            f_send.at[d],
            f_recv.at[d],
            seq=peer,
        ).wait_recv()
    early[2].wait()

    def feature(j):
        wide = sig[j].astype(jnp.float32)
        total = taps[j, pl.ds(0, 1), span(z, own)] * wide
        for offset in (1, 2):
            term = taps[j, pl.ds(offset, 1), span(z, own)] * pltpu.roll(wide, offset, 0)
            total = total + jnp.where(same[offset - 1], term, 0.0)
        return total

    mixed = feature(1) * feature(2)
    for load in loads[:4]:
        load.wait()
    both = jnp.concatenate([mixed.astype(jnp.bfloat16), fil[...]], axis=1)
    spec = bf_dot(high[...], both) + bf_dot(low[...], both)
    mix_cos, mix_sin = spec[:count, :own], spec[count:, :own]
    fil_cos, fil_sin = spec[:count, own:], spec[count:, own:]
    product = jnp.concatenate(
        [mix_cos * fil_cos - mix_sin * fil_sin, mix_cos * fil_sin + mix_sin * fil_cos], axis=0
    ).astype(jnp.bfloat16)
    conv = (bf_dot(high_t[...], product) + bf_dot(low_t[...], product)) * (1.0 / count)
    early[3].wait()
    for d in range(1, n):
        peer = lax.rem(z + n - d, n)
        sig_copy(1, d, peer, peer).wait_recv()
    gated = feature(0) * (conv + skip[:, span(z, own)] * mixed)
    g_send[...] = gated.astype(jnp.bfloat16)

    def column(shard):
        return g_all.at[:, span(x * n + shard, own)]

    for d in range(1, n):
        peer = lax.rem(z + d, n)
        copy = remote(
            g_send.at[span(peer, rows), :], column(z), b_send.at[d], b_recv.at[d], seq=peer
        )
        copy.start()
        sent.append(copy)
    g_all[:, span(x * n + z, own)] = g_send[span(z, rows), :]
    early[4].wait()
    acc[...] = residual[...].astype(jnp.float32)
    loads[4].wait()
    for d in range(1, n):
        peer = lax.rem(z + n - d, n)
        remote(
            g_send.at[span(peer, rows), :], column(peer), b_send.at[d], b_recv.at[d], seq=peer
        ).wait_recv()

    out_parts, head_parts = c_send.shape[1], d_send.shape[1]
    out_step, head_step = channels // out_parts, local_width // head_parts

    def out_part(i):
        acc[...] += bf_dot(g_all[:, span(i, out_step)], out_w[span(i, out_step), :])

    sent += pair_gather(g_all, x, m, channels, out_parts, c_send, c_recv, out_part)
    hidden = acc[...].astype(jnp.bfloat16)
    h_all[:, span(x, local_width)] = hidden
    written = [
        pltpu.make_async_copy(h_all.at[:, span(x, local_width)], hidden_out, local_sem.at[15])
    ]
    written[0].start()
    early[5].wait()
    squares[...] = jnp.zeros_like(squares)
    kv_acc[...] = jnp.zeros_like(kv_acc)
    loads[5].wait()
    loads[6].wait()

    def head_part(i):
        block = h_all[:, span(i, head_step)].astype(jnp.float32)
        squares[...] += jnp.sum(block * block, axis=1, keepdims=True)
        scaled = (block * gain[:, span(i, head_step)]).astype(jnp.bfloat16)
        n_all[:, span(i, head_step)] = scaled
        for j in (1, 2):
            kv_acc[j - 1] += bf_dot(scaled, head[j, span(i, head_step), :])

    sent += pair_gather(h_all, x, m, local_width, head_parts, d_send, d_recv, head_part)
    scale = lax.rsqrt(squares[:, :1] * (1.0 / width) + EPSILON)
    def kv_copy(d, part):
        return remote(
            kv.at[d - 1, part],
            kv.at[d, part],
            k_send.at[d, part],
            k_recv.at[d, part],
            seq=lax.rem(z + 1, n),
        )

    for part in range(2):
        kv[0, part] = (kv_acc[part] * scale).astype(jnp.bfloat16)

        @pl.when(z + 1 < n)
        def _(part=part):
            kv_copy(1, part).start()

    loads[7].wait()
    query = (bf_dot(n_all[...], head[0]) * scale).astype(jnp.bfloat16)
    own_ids = seg_wide[span(z, rows), :][:, :1]
    query_pos = z * rows + lax.broadcasted_iota(jnp.int32, (rows, rows), 0)
    allowed = []
    for d in range(reach + 1):
        shard = lax.max(z - d, 0)
        key_pos = (z - d) * rows + lax.broadcasted_iota(jnp.int32, (rows, rows), 1)
        ids = segs[:, span(shard, rows)].astype(jnp.float32)
        allowed.append((key_pos >= 0) & (key_pos <= query_pos) & (ids == own_ids))
    allowed = jnp.concatenate(allowed, axis=1)
    heads = [slice(h * DH, (h + 1) * DH) for h in range(channels // DH)]

    def scores(d):
        return [
            lax.dot_general(
                query[:, cols],
                kv[d, 0, :, cols],
                (((1,), (1,)), ((), ())),
                preferred_element_type=jnp.float32,
            )
            for cols in heads
        ]

    def receive(d, part):
        @pl.when(z >= d)
        def _():
            kv_copy(d, part).wait_recv()

        if d < reach:

            @pl.when(jnp.logical_and(z >= d, z + 1 < n))
            def _():
                kv_copy(d + 1, part).start()

    found = [scores(0)]
    for d in range(1, reach + 1):
        receive(d, 0)
        found.append(scores(d))
        if d < reach:
            receive(d, 1)
    weights = []
    for h in range(len(heads)):
        score = jnp.concatenate([block[h] for block in found], axis=1)
        score = jnp.where(allowed, score * (1.0 / math.sqrt(DH)), -1e30)
        weight = jnp.where(allowed, jnp.exp(score - jnp.max(score, axis=1, keepdims=True)), 0.0)
        mass = jnp.sum(weight, axis=1, keepdims=True)
        weights.append((weight.astype(jnp.bfloat16), mass))
    receive(reach, 1)
    for (weight, mass), cols in zip(weights, heads):
        values = jnp.concatenate([kv[d, 1, :, cols] for d in range(reach + 1)], axis=0)
        ctx[:, cols] = (bf_dot(weight, values) / mass).astype(jnp.bfloat16)
    written.append(pltpu.make_async_copy(ctx, context_out, local_sem.at[0]))
    written[1].start()
    for copy in sent:
        copy.wait_send()
    for d in range(1, reach + 1):
        for part in range(2):

            @pl.when(jnp.logical_and(z >= d - 1, z + 1 < n))
            def _(d=d, part=part):
                kv_copy(d, part).wait_send()

    for copy in written:
        copy.wait()


def aligned(
    branches,
    residual,
    segments,
    long_filter,
    short_taps,
    skip_gain,
    out_weight,
    norm_gain,
    head_weight,
):
    rows, _, channels = branches.shape
    local_width = residual.shape[1]
    n = lax.axis_size("seq")
    m = lax.axis_size("tp")
    own = channels // n
    count = rows * n
    width = head_weight.shape[0]
    reach = n // 2
    high, low = turn_tables(count)
    hbm = pl.BlockSpec(memory_space=pltpu.HBM)
    bf16, f32 = jnp.bfloat16, jnp.float32
    dma = pltpu.SemaphoreType.DMA
    return pl.pallas_call(
        functools.partial(layer_kernel, n, m),
        out_shape=(
            jax.ShapeDtypeStruct((rows, local_width), bf16),
            jax.ShapeDtypeStruct((rows, channels), bf16),
        ),
        in_specs=[hbm] * 13,
        out_specs=(hbm, hbm),
        scratch_shapes=[
            pltpu.VMEM((rows, channels), f32),
            pltpu.VMEM((rows, local_width), bf16),
            pltpu.VMEM((1, count), jnp.int32),
            pltpu.VMEM(short_taps.shape, f32),
            pltpu.VMEM((1, channels), f32),
            pltpu.VMEM((1, width), f32),
            pltpu.VMEM((rows, channels), bf16),
            pltpu.VMEM((rows, channels), bf16),
            pltpu.VMEM((3, count, own), bf16),
            pltpu.VMEM((count, own), bf16),
            pltpu.VMEM((2 * count, count), bf16),
            pltpu.VMEM((2 * count, count), bf16),
            pltpu.VMEM((count, 2 * count), bf16),
            pltpu.VMEM((count, 2 * count), bf16),
            pltpu.VMEM(out_weight.shape, bf16),
            pltpu.VMEM((3, width, channels), bf16),
            pltpu.VMEM((count, own), f32),
            pltpu.VMEM((count, own), bf16),
            pltpu.VMEM((rows, m * channels), bf16),
            pltpu.VMEM((rows, local_width), f32),
            pltpu.VMEM((rows, width), bf16),
            pltpu.VMEM((rows, width), bf16),
            pltpu.VMEM((rows, 128), f32),
            pltpu.VMEM((2, rows, channels), f32),
            pltpu.VMEM((reach + 1, 2, rows, channels), bf16),
            dma((16,)),
            dma((2, n)),
            dma((2, n)),
            dma((n,)),
            dma((n,)),
            dma((n,)),
            dma((n,)),
            dma((m, 2)),
            dma((m, 2)),
            dma((m, 4)),
            dma((m, 4)),
            dma((reach + 1, 2)),
            dma((reach + 1, 2)),
        ],
        compiler_params=pltpu.CompilerParams(
            collective_id=0, has_side_effects=True, vmem_limit_bytes=62 * 2**20
        ),
    )(
        jnp.swapaxes(branches, 0, 1),
        long_filter,
        residual,
        segments.reshape(1, -1),
        short_taps,
        skip_gain.reshape(1, -1),
        norm_gain.reshape(1, -1),
        high,
        low,
        np.ascontiguousarray(high.T),
        np.ascontiguousarray(low.T),
        out_weight,
        jnp.swapaxes(head_weight, 0, 1),
    )


def solution(mesh):
    placed = (
        P(("groups", "seq"), None, "tp"),
        P(("groups", "seq"), "tp"),
        P("groups"),
        P("seq", "tp"),
        P(None, None, "tp"),
        P("tp"),
        P(None, "tp"),
        P(),
        P(None, None, "tp"),
    )
    def chosen(*arrays):
        channels, rows = arrays[0].shape[2], arrays[0].shape[0]
        shards = lax.axis_size("seq")
        fits = channels % (shards * 128) == 0 and arrays[1].shape[1] % 512 == 0 and rows % 128 == 0 and shards * rows <= 1024
        fits = fits and shards % 2 == 0 and lax.axis_size("tp") % 2 == 0
        return aligned(*arrays) if fits else local(*arrays)

    return jax.shard_map(
        chosen,
        mesh=mesh,
        in_specs=placed,
        out_specs=(P(("groups", "seq"), "tp"), P(("groups", "seq"), "tp")),
        check_vma=False,
    )
```
